512 devices in a mesh: perm: 16 (over y, core), summa: 32 (over z, x).
Axes of the slice: x: 4, y: 8, z: 8, core: 2. Of those that a mesh axis runs over, the one named last changes fastest.
Arguments:
- amplitudes: bfloat16 [16, 1024, 1024], P('perm', None, 'summa'), may hold values from -6 to 6
- cycle_panels: bfloat16 [16, 128, 64, 1024], P('perm', None, 'summa'), may hold values from -0.75 to 0.75
- tile_mask: int32 [8, 2, 8, 8], replicated, may hold values 0 or 1
- panel_slot: int32 [16], replicated, may hold values from 0 to 15, each once
- window_blocks: int32 [4], replicated, may hold values from 0 to 7, as said below
- virt_energy: float32 [1024], replicated, may hold values from 0.5 to 3
- row_energy: float32 [8], replicated, may hold values from -2 to -0.5
- col_energy: float32 [64], P('summa'), may hold values from -2 to -0.5
Outputs:
- update: bfloat16 [1024, 8, 64, 1024], P('perm', None, 'summa')
The draws below stay inside these ranges and needn't reach their ends.
Inputs may be any that keep to these rules, and one draw needn't show every extreme that they name: `panel_slot`: a permutation: each of the 16 slots holds exactly one panel. `window_blocks`: 4 distinct tile numbers in no particular order; tile 0 and tile 8 - 1 are always among them.
All inputs are finite; a program needn't handle non-finite values.
Results may differ from the reference program's by a relative error of at most 0.001.
Values may be sent and summed in bfloat16 or wider, within the bound.
No kernel may reach another device: no remote copies, remote signals or barrier semaphores. Data moves between devices by JAX's collectives and lax.ppermute only.
A program may use at most 64 MiB of HBM per device.

```python
import jax
import jax.numpy as jnp
from jax import lax

TILE = 128
V = 1024
NVB = 8
OCC_ROW = 8
OCC_SUM = 2
WIN_BLOCKS = 4
OCC_COL = 64
PAIRS = 16
SLOTS = 16


def draw_window_blocks(key, part):
    key = jax.random.fold_in(key, 5)
    first_key, second_key = jax.random.split(key)
    middle = 1 + jax.random.permutation(first_key, NVB - 2)[:WIN_BLOCKS - 2]
    picks = jnp.concatenate([jnp.array([0, NVB - 1], dtype=jnp.int32), middle.astype(jnp.int32)])
    order = jax.random.permutation(second_key, WIN_BLOCKS)
    return picks[order].astype(jnp.int32)


def set_ends(values, key, low, high):
    place = [jax.random.randint(jax.random.fold_in(key, axis), (), 0, length) for axis, length in enumerate(values.shape)]
    widest = values.shape.index(max(values.shape))
    neighbour = place[:widest] + [(place[widest] + 1) % values.shape[widest]] + place[widest + 1:]
    return values.at[tuple(place)].set(low).at[tuple(neighbour)].set(high)


def levels(stream_key, shape, cuts, smallest, top_value):
    loudness, own = 1.0, jax.random.fold_in(stream_key, 6)
    for position, parts in cuts:
        draws = jnp.exp(jax.random.uniform(jax.random.fold_in(own, position), (parts,), jnp.float32, smallest / len(cuts), top_value / len(cuts)))
        loudness = loudness * jnp.repeat(draws, shape[position] // parts).reshape([-1 if axis == position else 1 for axis in range(len(shape))])
    return loudness


def centred(rng, shape, spread, most, cuts=(), kind=jnp.bfloat16):
    drawn = jax.random.normal(rng, shape, jnp.float32) * spread
    if len(cuts) > 0:
        drawn = levels(rng, shape, cuts, -0.22, 0.18) * drawn
    return jnp.clip(drawn, min=-most, max=most).astype(kind)


def setup_inputs(seed: int = 0) -> dict:
    seeds = jax.random.split(jax.random.key(seed), 9)
    amplitudes = centred(seeds[0], (PAIRS, V, V), 1.0, 6.0, ((0, 16), (2, 32)))
    cycle_panels = centred(seeds[1], (SLOTS, TILE, OCC_COL, V), (OCC_SUM * WIN_BLOCKS * TILE // 16) ** -0.5, 0.75, ((0, 16), (2, 32)))
    tile_mask = set_ends((jax.random.randint(seeds[2], (OCC_ROW, OCC_SUM, NVB, NVB), 0, 2) < 1).astype(jnp.int32), jax.random.fold_in(seeds[2], 1), 0, 1)
    panel_slot = jax.random.permutation(seeds[3], SLOTS).astype(jnp.int32)
    window_blocks = draw_window_blocks(jax.random.fold_in(seeds[8], 71), 0)
    virt_energy = jnp.clip(jax.random.uniform(seeds[5], (V,), jnp.float32, 0.5, 3.0), 0.5, 3.0)
    row_energy = jnp.clip(jax.random.uniform(seeds[6], (OCC_ROW,), jnp.float32, -2.0, -0.5), -2.0, -0.5)
    col_energy = jnp.clip(-2.0 + 1.5 * jax.random.uniform(seeds[7], (OCC_COL,), jnp.float32) ** levels(seeds[7], (OCC_COL,), ((0, 32),), -0.2, 0.2), -2.0, -0.5)
    return {"amplitudes": amplitudes, "cycle_panels": cycle_panels, "tile_mask": tile_mask, "panel_slot": panel_slot, "window_blocks": window_blocks, "virt_energy": virt_energy, "row_energy": row_energy, "col_energy": col_energy}


def reference(amplitudes, cycle_panels, tile_mask, panel_slot, window_blocks, virt_energy, row_energy, col_energy):
    blocked = amplitudes.reshape(OCC_ROW, OCC_SUM, V, NVB, TILE)
    selected = jnp.take(blocked, window_blocks, axis=3)
    mask_window = jnp.take(tile_mask, window_blocks, axis=3)
    mask_rows = jnp.repeat(mask_window, TILE, axis=2)
    masked = selected * mask_rows[..., None].astype(jnp.bfloat16)
    chosen = jnp.take(panel_slot.reshape(OCC_SUM, NVB), window_blocks, axis=1)
    panels = jnp.take(cycle_panels, chosen.reshape(-1), axis=0)
    panels = panels.reshape(OCC_SUM, WIN_BLOCKS, TILE, OCC_COL, V).astype(jnp.float32)
    a_blocks = jnp.moveaxis(masked.reshape(OCC_ROW, OCC_SUM, NVB, TILE, WIN_BLOCKS, TILE), 2, 0)
    energy_blocks = virt_energy.reshape(NVB, TILE)

    def one_block(pieces):
        a_block, energy = pieces
        cycle_term = jnp.einsum('ikawc,kwcjb->aijb', a_block.astype(jnp.float32), panels)
        denominator = (energy[:, None, None, None] + virt_energy[None, None, None, :]
                       - row_energy[None, :, None, None] - col_energy[None, None, :, None])
        return (cycle_term / denominator).astype(jnp.bfloat16)

    result = lax.map(one_block, (a_blocks, energy_blocks))
    return result.reshape(V, OCC_ROW, OCC_COL, V)
```

```python
import jax
import jax.numpy as jnp
from jax import lax
from jax.experimental import pallas as pl
from jax.experimental.pallas import tpu as pltpu
from jax.sharding import PartitionSpec as P

CHIPS_Y, CORES, CHIPS_Z, CHIPS_X = 8, 2, 8, 4


def along_y(value, step):
    pairs = [
        (y * CORES + core, (y + step) % CHIPS_Y * CORES + core)
        for y in range(CHIPS_Y)
        for core in range(CORES)
    ]
    return lax.ppermute(value, "perm", pairs)


def other_core(value):
    pairs = [(p, p ^ 1) for p in range(CHIPS_Y * CORES)]
    return lax.ppermute(value, "perm", pairs)


def along_z(value, step):
    pairs = [
        (z * CHIPS_X + x, (z + step) % CHIPS_Z * CHIPS_X + x)
        for z in range(CHIPS_Z)
        for x in range(CHIPS_X)
    ]
    return lax.ppermute(value, "summa", pairs)


def along_x(value, step):
    pairs = [
        (z * CHIPS_X + x, z * CHIPS_X + (x + step) % CHIPS_X)
        for z in range(CHIPS_Z)
        for x in range(CHIPS_X)
    ]
    return lax.ppermute(value, "summa", pairs)


def contract_kernel(chosen, lhs, slots, row_energy, col_energy, out, panels, sems):
    count, width = chosen.shape[0], slots.shape[1]
    copies = [
        pltpu.make_async_copy(
            slots.at[chosen[m]], panels.at[pl.ds(m * width, width)], sems.at[m]
        )
        for m in range(count)
    ]
    for copy in copies:
        copy.start()
    for copy in copies:
        copy.wait()
    term = jnp.dot(lhs[...], panels[...], preferred_element_type=jnp.float32)
    out[...] = (term / (row_energy[...] + col_energy[...])).astype(out.dtype)


def contract(chosen, lhs, slots, row_energy, col_energy):
    rows, depth = lhs.shape
    width_virt = slots.shape[2]
    vmem = pl.BlockSpec(memory_space=pltpu.VMEM)
    return pl.pallas_call(
        contract_kernel,
        out_shape=jax.ShapeDtypeStruct((rows, width_virt), jnp.bfloat16),
        in_specs=[
            pl.BlockSpec(memory_space=pltpu.SMEM),
            vmem,
            pl.BlockSpec(memory_space=pltpu.HBM),
            vmem,
            vmem,
        ],
        out_specs=vmem,
        scratch_shapes=[
            pltpu.VMEM((depth, width_virt), jnp.bfloat16),
            pltpu.SemaphoreType.DMA((chosen.shape[0],)),
        ],
        compiler_params=pltpu.CompilerParams(vmem_limit_bytes=32 * 1024 * 1024),
    )(chosen, lhs, slots, row_energy, col_energy)


def body(
    amplitudes,
    cycle_panels,
    tile_mask,
    panel_slot,
    window_blocks,
    virt_energy,
    row_energy,
    col_energy,
):
    _, tile_width, col_local, width_virt = cycle_panels.shape
    c_local = amplitudes.shape[2]
    occ_rows, occ_summed, block_count, _ = tile_mask.shape
    window_count = window_blocks.shape[0]
    p, s = lax.axis_index("perm"), lax.axis_index("summa")
    y, core = p >> 1, p & 1
    z, x = s >> 2, s & 3

    by_col = jnp.swapaxes(cycle_panels[0], 0, 1)
    gathered = [lax.all_gather(by_col[j], "perm", axis=0) for j in range(col_local)]

    tiles = amplitudes[0].T.reshape(c_local, block_count, tile_width)
    rows_of = []
    for step in range(CHIPS_Y):
        tile = lax.dynamic_index_in_dim(tiles, (y + step) & (CHIPS_Y - 1), axis=1, keepdims=False)
        rows_of.append(along_y(tile, step) if step else tile)
    own = jnp.stack(rows_of)
    own = jnp.take(own, (y - jnp.arange(occ_rows)) & (CHIPS_Y - 1), axis=0)

    from_z = {0: own}
    for step in range(1, CHIPS_Z // 2 + 1):
        from_z[step] = along_z(from_z[step - 1], 1)
        if step < CHIPS_Z // 2:
            from_z[CHIPS_Z - step] = along_z(from_z[(CHIPS_Z - step + 1) % CHIPS_Z], -1)
    stacked = jnp.stack([from_z[step] for step in range(CHIPS_Z)])
    window = jnp.take(stacked, (z - window_blocks) & (CHIPS_Z - 1), axis=0)

    from_x = [window, along_x(window, 1), along_x(window, 2), along_x(window, -1)]
    window = jnp.take(jnp.stack(from_x), (x - jnp.arange(CHIPS_X)) & (CHIPS_X - 1), axis=0)

    other = other_core(window)
    both = jnp.stack([jnp.where(core == 0, window, other), jnp.where(core == 0, other, window)])
    half = tile_width // CORES
    both = lax.dynamic_slice_in_dim(both, core * half, half, axis=5)
    mask = lax.dynamic_index_in_dim(tile_mask, y, axis=2, keepdims=False)
    mask = jnp.take(mask, window_blocks, axis=2).astype(jnp.bfloat16)
    lhs = jnp.transpose(both, (5, 3, 0, 2, 1, 4)) * mask[None, :, :, :, None, None]
    lhs = lhs.reshape(half * occ_rows, occ_summed * window_count * tile_width)

    chosen = jnp.take(panel_slot.reshape(occ_summed, block_count), window_blocks, axis=1)
    chosen = chosen.reshape(-1)
    row_virt = lax.dynamic_slice_in_dim(virt_energy, p * half, half)
    rows = (row_virt[:, None] - row_energy[None, :]).reshape(-1, 1)
    results = [
        contract(chosen, lhs, gathered[j], rows, (virt_energy - col_energy[j])[None, :])
        for j in range(col_local)
    ]
    return jnp.stack(results, axis=1).reshape(half, occ_rows, col_local, width_virt)


def solution(mesh):
    in_specs = (
        P("perm", None, "summa"),
        P("perm", None, "summa", None),
        P(),
        P(),
        P(),
        P(),
        P(),
        P("summa"),
    )
    out_specs = P("perm", None, "summa", None)
    return jax.shard_map(body, mesh=mesh, in_specs=in_specs, out_specs=out_specs, check_vma=False)
```

```python
import jax
import jax.numpy as jnp
from jax import lax
from jax.experimental import pallas as pl
from jax.experimental.pallas import tpu as pltpu
from jax.sharding import PartitionSpec as P

CHIPS_Z, CHIPS_X = 8, 4
ALONG_Z = [[z * CHIPS_X + x for z in range(CHIPS_Z)] for x in range(CHIPS_X)]
ALONG_X = [[z * CHIPS_X + x for x in range(CHIPS_X)] for z in range(CHIPS_Z)]
MIB = 1024 * 1024
LANES = 128


def gather_by_exchange(value, groups):
    count = len(groups[0])
    copies = jnp.broadcast_to(value[None], (count, *value.shape))
    return lax.all_to_all(copies, "summa", 0, 0, axis_index_groups=groups, tiled=True)


def rows_kernel(mask, window, row_tile, tiles, out, rows):
    x_count, windows, occ_rows, c_local, lanes = tiles.shape
    blocks = lax.axis_size("perm") // 2
    summed = mask.shape[0] // (occ_rows * blocks * blocks)
    half, width = lanes // summed, x_count * c_local
    for i in range(occ_rows):
        for w in range(windows):
            tile = tiles[:, w, i].reshape(width, lanes).astype(jnp.float32).T
            for k in range(summed):
                keep = mask[((i * summed + k) * blocks + row_tile[0]) * blocks + window[w]]
                rows[:, i, pl.ds((k * windows + w) * width, width)] = (
                    tile[k * half : (k + 1) * half] * keep.astype(jnp.float32)
                )
    out[...] = rows[...].reshape(out.shape).astype(out.dtype)


def amplitude_rows(tile_mask, window, row_tile, tiles):
    x_count, windows, occ_rows, c_local, lanes = tiles.shape
    summed = tile_mask.shape[1]
    smem = pl.BlockSpec(memory_space=pltpu.SMEM)
    half, depth = lanes // summed, summed * windows * x_count * c_local
    return pl.pallas_call(
        rows_kernel,
        out_shape=jax.ShapeDtypeStruct((half * occ_rows, depth), jnp.bfloat16),
        in_specs=[smem, smem, smem, pl.BlockSpec(memory_space=pltpu.VMEM)],
        out_specs=pl.BlockSpec(memory_space=pltpu.VMEM),
        scratch_shapes=[pltpu.VMEM((half, occ_rows, depth), jnp.float32)],
        compiler_params=pltpu.CompilerParams(vmem_limit_bytes=32 * MIB),
    )(tile_mask.reshape(-1), window, row_tile, tiles)


def contract_kernel(panel_slot, window, lhs, row_energy, col_energy, *refs):
    *panels, out, pairs = refs
    rows = lhs.shape[0]
    cols = panels[0].shape[1]
    for j in range(cols):
        rhs = jnp.concatenate([panel[0, j] for panel in panels], axis=0)
        term = jnp.dot(lhs[...], rhs, preferred_element_type=jnp.float32)
        term = term / (row_energy[...] + col_energy[pl.ds(j, 1), :])
        for n in range(pairs.shape[0]):
            pairs[n, pl.ds(j, rows, stride=cols), :] = term[:, n * LANES : (n + 1) * LANES]
    flat = out.reshape(rows * cols, out.shape[2])
    for n in range(pairs.shape[0]):
        flat[:, pl.ds(n * LANES, LANES)] = pairs[n].astype(out.dtype)


def contract(panel_slot, window, lhs, row_energy, col_energy, slots, lanes):
    rows, depth = lhs.shape
    _, cols, width, width_virt = slots.shape
    windows = window.shape[0]
    summed = depth // (width * windows)
    blocks = panel_slot.shape[0] // summed

    def panel_spec(k, w):
        def place(n, panel_slot, window):
            return panel_slot[k * blocks + window[w]], 0, 0, n

        return pl.BlockSpec((1, cols, width, lanes), place)

    return pl.pallas_call(
        contract_kernel,
        out_shape=jax.ShapeDtypeStruct((rows, cols, width_virt), jnp.bfloat16),
        grid_spec=pltpu.PrefetchScalarGridSpec(
            num_scalar_prefetch=2,
            grid=(width_virt // lanes,),
            in_specs=[
                pl.BlockSpec((rows, depth), lambda n, *_: (0, 0)),
                pl.BlockSpec((rows, 1), lambda n, *_: (0, 0)),
                pl.BlockSpec((cols, lanes), lambda n, *_: (0, n)),
                *[panel_spec(k, w) for k in range(summed) for w in range(windows)],
            ],
            out_specs=pl.BlockSpec((rows, cols, lanes), lambda n, *_: (0, 0, n)),
            scratch_shapes=[pltpu.VMEM((lanes // LANES, rows * cols, LANES), jnp.float32)],
        ),
        compiler_params=pltpu.CompilerParams(vmem_limit_bytes=56 * MIB),
    )(panel_slot, window, lhs, row_energy, col_energy, *[slots] * (summed * windows))


def body(
    amplitudes,
    cycle_panels,
    tile_mask,
    panel_slot,
    window_blocks,
    virt_energy,
    row_energy,
    col_energy,
):
    _, _, col_local, width_virt = cycle_panels.shape
    c_local = amplitudes.shape[2]
    occ_rows, occ_summed = tile_mask.shape[:2]
    perm_count = lax.axis_size("perm")
    a_local = amplitudes.shape[1] // perm_count
    p = lax.axis_index("perm")

    slots = lax.all_gather(jnp.swapaxes(cycle_panels[0], 0, 1), "perm", axis=0)

    blocks = jnp.swapaxes(amplitudes[0].T.reshape(c_local, perm_count, a_local), 0, 1)
    blocks = lax.all_to_all(blocks, "perm", 0, 0, tiled=True)
    blocks = blocks.reshape(occ_rows, occ_summed, c_local, a_local)
    blocks = jnp.concatenate([blocks[:, k] for k in range(occ_summed)], axis=-1)
    tiles = gather_by_exchange(blocks, ALONG_Z)
    tiles = jnp.stack(
        [lax.dynamic_index_in_dim(tiles, window_blocks[w], 0, False) for w in range(window_blocks.shape[0])]
    )
    tiles = gather_by_exchange(tiles, ALONG_X)
    lhs = amplitude_rows(tile_mask, window_blocks, (p >> 1).reshape(1), tiles)

    row_virt = lax.dynamic_slice_in_dim(virt_energy, p * a_local, a_local)
    rows = (row_virt[:, None] - row_energy[None, :]).reshape(-1, 1)
    columns = virt_energy[None, :] - col_energy[:, None]
    result = contract(panel_slot, window_blocks, lhs, rows, columns, slots, 256)
    return result.reshape(a_local, occ_rows, col_local, width_virt)


def solution(mesh):
    in_specs = (
        P("perm", None, "summa"),
        P("perm", None, "summa", None),
        P(),
        P(),
        P(),
        P(),
        P(),
        P("summa"),
    )
    out_specs = P("perm", None, "summa", None)
    return jax.shard_map(body, mesh=mesh, in_specs=in_specs, out_specs=out_specs, check_vma=False)
```

```python
import jax
import jax.numpy as jnp
from jax import lax
from jax.experimental import pallas as pl
from jax.experimental.pallas import tpu as pltpu
from jax.sharding import PartitionSpec as P

CHIPS_Z, CHIPS_X = 8, 4
ALONG_Z = [[z * CHIPS_X + x for z in range(CHIPS_Z)] for x in range(CHIPS_X)]
ALONG_X = [[z * CHIPS_X + x for x in range(CHIPS_X)] for z in range(CHIPS_Z)]
MIB = 1024 * 1024
LANES = 128


def gather_by_exchange(value, groups):
    count = len(groups[0])
    copies = jnp.broadcast_to(value[None], (count, *value.shape))
    return lax.all_to_all(copies, "summa", 0, 0, axis_index_groups=groups, tiled=True)


def along_x(value, step):
    pairs = [(group[x], group[(x + step) % CHIPS_X]) for group in ALONG_X for x in range(CHIPS_X)]
    return lax.ppermute(value, "summa", pairs)


def rows_kernel(mask, window, place, own, left, right, far_low, far_high, out, tiles, rows):
    windows, occ_rows, c_local, lanes = own.shape
    x_count = tiles.shape[0]
    blocks = lax.axis_size("perm") // 2
    summed = mask.shape[0] // (occ_rows * blocks * blocks)
    half, width = lanes // summed, x_count * c_local
    row_tile, x = place[0], place[1]
    tiles[x] = own[...]
    tiles[(x + x_count - 1) & (x_count - 1)] = left[...]
    tiles[(x + 1) & (x_count - 1)] = right[...]
    far = (x + 2) & (x_count - 1)
    tiles[far, :, pl.ds(0, occ_rows // 2)] = far_low[...]
    tiles[far, :, pl.ds(occ_rows // 2, occ_rows // 2)] = far_high[...]
    for i in range(occ_rows):
        for w in range(windows):
            tile = tiles[:, w, i].reshape(width, lanes).astype(jnp.float32).T
            for k in range(summed):
                keep = mask[((i * summed + k) * blocks + row_tile) * blocks + window[w]]
                rows[:, i, pl.ds((k * windows + w) * width, width)] = (
                    tile[k * half : (k + 1) * half] * keep.astype(jnp.float32)
                )
    out[...] = rows[...].reshape(out.shape).astype(out.dtype)


def amplitude_rows(tile_mask, window, place, parts):
    windows, occ_rows, c_local, lanes = parts[0].shape
    summed = tile_mask.shape[1]
    smem, vmem = pl.BlockSpec(memory_space=pltpu.SMEM), pl.BlockSpec(memory_space=pltpu.VMEM)
    half, depth = lanes // summed, summed * windows * CHIPS_X * c_local
    return pl.pallas_call(
        rows_kernel,
        out_shape=jax.ShapeDtypeStruct((half * occ_rows, depth), jnp.bfloat16),
        in_specs=[smem, smem, smem] + [vmem] * len(parts),
        out_specs=vmem,
        scratch_shapes=[
            pltpu.VMEM((CHIPS_X, *parts[0].shape), jnp.bfloat16),
            pltpu.VMEM((half, occ_rows, depth), jnp.float32),
        ],
        compiler_params=pltpu.CompilerParams(vmem_limit_bytes=32 * MIB),
    )(tile_mask.reshape(-1), window, place, *parts)


def contract_kernel(panel_slot, window, lhs, row_energy, col_energy, slots, out, panels, pairs, done, came, left):
    rows, depth = lhs.shape
    chunks, cols, count, width, lanes = panels.shape
    windows = window.shape[0]
    summed = count // windows
    blocks = panel_slot.shape[0] // summed
    fetches = [
        [
            pltpu.make_async_copy(
                slots.at[panel_slot[k * blocks + window[w]], :, :, pl.ds(n * lanes, lanes)],
                panels.at[n, :, k * windows + w],
                came.at[n, k * windows + w],
            )
            for k in range(summed)
            for w in range(windows)
        ]
        for n in range(chunks)
    ]
    for fetch in sum(fetches, []):
        fetch.start()
    stores = []
    for n in range(chunks):
        for fetch in fetches[n]:
            fetch.wait()
        for j in range(cols):
            term = jnp.dot(
                lhs[...], panels[n, j].reshape(depth, lanes), preferred_element_type=jnp.float32
            )
            gap = row_energy[...] + col_energy[pl.ds(j, 1), pl.ds(n * lanes, lanes)]
            guess = pl.reciprocal(gap, approx=True)
            term = term * (guess * (2.0 - gap * guess))
            for part in range(lanes // LANES):
                pairs[part, pl.ds(j, rows, stride=cols), :] = term[:, part * LANES : (part + 1) * LANES]
        flat = done.at[n].reshape(rows * cols, lanes)
        for part in range(lanes // LANES):
            flat[:, pl.ds(part * LANES, LANES)] = pairs[part].astype(out.dtype)
        stores.append(
            pltpu.make_async_copy(done.at[n], out.at[:, :, pl.ds(n * lanes, lanes)], left.at[n])
        )
        stores[-1].start()
    for store in stores:
        store.wait()


def contract(panel_slot, window, lhs, row_energy, col_energy, slots, lanes):
    rows, depth = lhs.shape
    _, cols, width, width_virt = slots.shape
    count, chunks = depth // width, width_virt // lanes
    smem, vmem = pl.BlockSpec(memory_space=pltpu.SMEM), pl.BlockSpec(memory_space=pltpu.VMEM)
    hbm = pl.BlockSpec(memory_space=pltpu.HBM)
    return pl.pallas_call(
        contract_kernel,
        out_shape=jax.ShapeDtypeStruct((rows, cols, width_virt), jnp.bfloat16),
        in_specs=[smem, smem, vmem, vmem, vmem, hbm],
        out_specs=hbm,
        scratch_shapes=[
            pltpu.VMEM((chunks, cols, count, width, lanes), jnp.bfloat16),
            pltpu.VMEM((lanes // LANES, rows * cols, LANES), jnp.float32),
            pltpu.VMEM((chunks, rows, cols, lanes), jnp.bfloat16),
            pltpu.SemaphoreType.DMA((chunks, count)),
            pltpu.SemaphoreType.DMA((chunks,)),
        ],
        compiler_params=pltpu.CompilerParams(vmem_limit_bytes=56 * MIB),
    )(panel_slot, window, lhs, row_energy, col_energy, slots)


def body(
    amplitudes,
    cycle_panels,
    tile_mask,
    panel_slot,
    window_blocks,
    virt_energy,
    row_energy,
    col_energy,
):
    _, _, col_local, width_virt = cycle_panels.shape
    c_local = amplitudes.shape[2]
    occ_rows, occ_summed = tile_mask.shape[:2]
    perm_count = lax.axis_size("perm")
    a_local = amplitudes.shape[1] // perm_count
    p = lax.axis_index("perm")

    slots = lax.all_gather(jnp.swapaxes(cycle_panels[0], 0, 1), "perm", axis=0)

    blocks = jnp.swapaxes(amplitudes[0].T.reshape(c_local, perm_count, a_local), 0, 1)
    blocks = lax.all_to_all(blocks, "perm", 0, 0, tiled=True)
    blocks = blocks.reshape(occ_rows, occ_summed, c_local, a_local)
    blocks = jnp.concatenate([blocks[:, k] for k in range(occ_summed)], axis=-1)
    tiles = gather_by_exchange(blocks, ALONG_Z)
    tiles = jnp.stack(
        [lax.dynamic_index_in_dim(tiles, window_blocks[w], 0, False) for w in range(window_blocks.shape[0])]
    )
    half_rows = occ_rows // 2
    parts = (
        tiles,
        along_x(tiles, 1),
        along_x(tiles, -1),
        along_x(tiles[:, :half_rows], 2),
        along_x(tiles[:, half_rows:], -2),
    )
    place = jnp.stack([p >> 1, lax.axis_index("summa") & (CHIPS_X - 1)])
    lhs = amplitude_rows(tile_mask, window_blocks, place, parts)

    row_virt = lax.dynamic_slice_in_dim(virt_energy, p * a_local, a_local)
    rows = (row_virt[:, None] - row_energy[None, :]).reshape(-1, 1)
    columns = virt_energy[None, :] - col_energy[:, None]
    result = contract(panel_slot, window_blocks, lhs, rows, columns, slots, 256)
    return result.reshape(a_local, occ_rows, col_local, width_virt)


def solution(mesh):
    in_specs = (
        P("perm", None, "summa"),
        P("perm", None, "summa", None),
        P(),
        P(),
        P(),
        P(),
        P(),
        P("summa"),
    )
    out_specs = P("perm", None, "summa", None)
    return jax.shard_map(body, mesh=mesh, in_specs=in_specs, out_specs=out_specs, check_vma=False)
```

```python
import jax
import jax.numpy as jnp
from jax import lax
from jax.experimental import pallas as pl
from jax.experimental.pallas import tpu as pltpu
from jax.sharding import PartitionSpec as P

CHIPS_Z, CHIPS_X = 8, 4
ALONG_Z = [[z * CHIPS_X + x for z in range(CHIPS_Z)] for x in range(CHIPS_X)]
ALONG_X = [[z * CHIPS_X + x for x in range(CHIPS_X)] for z in range(CHIPS_Z)]
MIB = 1024 * 1024
LANES, MXU = 128, 256


def gather_by_exchange(value, groups):
    count = len(groups[0])
    copies = jnp.broadcast_to(value[None], (count, *value.shape))
    return lax.all_to_all(copies, "summa", 0, 0, axis_index_groups=groups, tiled=True)


def rows_kernel(mask, window, row_tile, *refs):
    *parts, out, rows = refs
    x_count, windows, _, c_local, lanes = parts[0].shape
    half, occ_rows, _ = rows.shape
    blocks = lax.axis_size("perm") // 2
    summed, width = lanes // half, x_count * c_local
    i = 0
    for part in parts:
        for row in range(part.shape[2]):
            for w in range(windows):
                tile = part[:, w, row].reshape(width, lanes).astype(jnp.float32).T
                for k in range(summed):
                    keep = mask[((i * summed + k) * blocks + row_tile[0]) * blocks + window[w]]
                    rows[:, i, pl.ds((k * windows + w) * width, width)] = (
                        tile[k * half : (k + 1) * half] * keep.astype(jnp.float32)
                    )
            i += 1
    out[...] = rows[...].reshape(out.shape).astype(out.dtype)


def amplitude_rows(tile_mask, window, row_tile, parts):
    x_count, windows, _, c_local, lanes = parts[0].shape
    occ_rows, summed = tile_mask.shape[:2]
    smem, vmem = pl.BlockSpec(memory_space=pltpu.SMEM), pl.BlockSpec(memory_space=pltpu.VMEM)
    half, depth = lanes // summed, summed * windows * x_count * c_local
    return pl.pallas_call(
        rows_kernel,
        out_shape=jax.ShapeDtypeStruct((half * occ_rows, depth), jnp.bfloat16),
        in_specs=[smem, smem, smem] + [vmem] * len(parts),
        out_specs=vmem,
        scratch_shapes=[pltpu.VMEM((half, occ_rows, depth), jnp.float32)],
        compiler_params=pltpu.CompilerParams(vmem_limit_bytes=56 * MIB),
    )(tile_mask.reshape(-1), window, row_tile, *parts)


def contract_kernel(panel_slot, window, lhs, row_energy, col_energy, slots, out, panels, pairs, done, came, left):
    rows, depth = lhs.shape
    chunks, cols, count, width, lanes = panels.shape
    windows = window.shape[0]
    summed = count // windows
    blocks = panel_slot.shape[0] // summed
    fetches = [
        [
            pltpu.make_async_copy(
                slots.at[panel_slot[k * blocks + window[w]], :, :, pl.ds(n * lanes, lanes)],
                panels.at[n, :, k * windows + w],
                came.at[n, k * windows + w],
            )
            for k in range(summed)
            for w in range(windows)
        ]
        for n in range(chunks)
    ]
    for fetch in sum(fetches, []):
        fetch.start()
    stores = []
    for n in range(chunks):
        for fetch in fetches[n]:
            fetch.wait()
        for first in range(0, lanes, MXU):
            for j in range(cols):
                term = jnp.dot(
                    lhs[...],
                    panels[n, j, :, :, pl.ds(first, MXU)].reshape(depth, MXU),
                    preferred_element_type=jnp.float32,
                )
                gap = row_energy[...] + col_energy[pl.ds(j, 1), pl.ds(n * lanes + first, MXU)]
                guess = pl.reciprocal(gap, approx=True)
                term = term * (guess * (2.0 - gap * guess))
                for part in range(MXU // LANES):
                    pairs[first // LANES + part, pl.ds(j, rows, stride=cols), :] = term[
                        :, part * LANES : (part + 1) * LANES
                    ]
        flat = done.at[n].reshape(rows * cols, lanes)
        for part in range(lanes // LANES):
            flat[:, pl.ds(part * LANES, LANES)] = pairs[part].astype(out.dtype)
        stores.append(
            pltpu.make_async_copy(done.at[n], out.at[:, :, pl.ds(n * lanes, lanes)], left.at[n])
        )
        stores[-1].start()
    for store in stores:
        store.wait()


def contract(panel_slot, window, lhs, row_energy, col_energy, slots, lanes):
    rows, depth = lhs.shape
    _, cols, width, width_virt = slots.shape
    count, chunks = depth // width, width_virt // lanes
    smem, vmem = pl.BlockSpec(memory_space=pltpu.SMEM), pl.BlockSpec(memory_space=pltpu.VMEM)
    hbm = pl.BlockSpec(memory_space=pltpu.HBM)
    return pl.pallas_call(
        contract_kernel,
        out_shape=jax.ShapeDtypeStruct((rows, cols, width_virt), jnp.bfloat16),
        in_specs=[smem, smem, vmem, vmem, vmem, hbm],
        out_specs=hbm,
        scratch_shapes=[
            pltpu.VMEM((chunks, cols, count, width, lanes), jnp.bfloat16),
            pltpu.VMEM((lanes // LANES, rows * cols, LANES), jnp.float32),
            pltpu.VMEM((chunks, rows, cols, lanes), jnp.bfloat16),
            pltpu.SemaphoreType.DMA((chunks, count)),
            pltpu.SemaphoreType.DMA((chunks,)),
        ],
        compiler_params=pltpu.CompilerParams(vmem_limit_bytes=56 * MIB),
    )(panel_slot, window, lhs, row_energy, col_energy, slots)


def body(
    amplitudes,
    cycle_panels,
    tile_mask,
    panel_slot,
    window_blocks,
    virt_energy,
    row_energy,
    col_energy,
):
    _, _, col_local, width_virt = cycle_panels.shape
    c_local = amplitudes.shape[2]
    occ_rows, occ_summed = tile_mask.shape[:2]
    perm_count = lax.axis_size("perm")
    a_local = amplitudes.shape[1] // perm_count
    p = lax.axis_index("perm")

    slots = lax.all_gather(jnp.swapaxes(cycle_panels[0], 0, 1), "perm", axis=0)

    blocks = jnp.swapaxes(amplitudes[0].T.reshape(c_local, perm_count, a_local), 0, 1)
    blocks = lax.all_to_all(blocks, "perm", 0, 0, tiled=True)
    blocks = blocks.reshape(occ_rows, occ_summed, c_local, a_local)
    blocks = jnp.concatenate([blocks[:, k] for k in range(occ_summed)], axis=-1)
    parts = []
    for some in jnp.split(blocks, 2):
        tiles = gather_by_exchange(some, ALONG_Z)
        tiles = [lax.dynamic_index_in_dim(tiles, window_blocks[w], 0, False) for w in range(window_blocks.shape[0])]
        parts.append(gather_by_exchange(jnp.stack(tiles), ALONG_X))
    lhs = amplitude_rows(tile_mask, window_blocks, (p >> 1).reshape(1), parts)

    row_virt = lax.dynamic_slice_in_dim(virt_energy, p * a_local, a_local)
    rows = (row_virt[:, None] - row_energy[None, :]).reshape(-1, 1)
    columns = virt_energy[None, :] - col_energy[:, None]
    result = contract(panel_slot, window_blocks, lhs, rows, columns, slots, 512)
    return result.reshape(a_local, occ_rows, col_local, width_virt)


def solution(mesh):
    in_specs = (
        P("perm", None, "summa"),
        P("perm", None, "summa", None),
        P(),
        P(),
        P(),
        P(),
        P(),
        P("summa"),
    )
    out_specs = P("perm", None, "summa", None)
    return jax.shard_map(body, mesh=mesh, in_specs=in_specs, out_specs=out_specs, check_vma=False)
```

```python
import jax
import jax.numpy as jnp
from jax import lax
from jax.experimental import pallas as pl
from jax.experimental.pallas import tpu as pltpu
from jax.sharding import PartitionSpec as P

CHIPS_Z, CHIPS_X = 8, 4
ALONG_Z = [[z * CHIPS_X + x for z in range(CHIPS_Z)] for x in range(CHIPS_X)]
ALONG_X = [[z * CHIPS_X + x for x in range(CHIPS_X)] for z in range(CHIPS_Z)]
MIB = 1024 * 1024
LANES, MXU = 128, 256


def gather_by_exchange(value, groups):
    count = len(groups[0])
    copies = jnp.broadcast_to(value[None], (count, *value.shape))
    return lax.all_to_all(copies, "summa", 0, 0, axis_index_groups=groups, tiled=True)


def build_rows(mask, window, row_tile, tiles, rows, lhs):
    x_count, windows, occ_rows, c_local, lanes = tiles.shape
    half, width = rows.shape[0], x_count * c_local
    summed = lanes // half
    for i in range(occ_rows):
        for w in range(windows):
            tile = tiles[:, w, i].reshape(width, lanes).astype(jnp.float32).T
            for k in range(summed):
                keep = mask[i * summed + k, row_tile[0], window[w]].astype(jnp.float32)
                rows[:, i, pl.ds((k * windows + w) * width, width)] = (
                    tile[k * half : (k + 1) * half] * keep
                )
    lhs[...] = rows[...].reshape(lhs.shape).astype(lhs.dtype)


def contract_kernel(
    panel_slot, window, mask, row_tile, tiles_in, row_energy, col_energy, slots, out,
    tiles, row_part, col_part, panels, rows, lhs, pairs, done, first_came, came, left,
):
    depth = lhs.shape[1]
    chunks, cols, count, width, lanes = panels.shape
    row_count = lhs.shape[0]
    windows = window.shape[0]
    summed = count // windows
    blocks = panel_slot.shape[0] // summed
    fetches = [
        [
            pltpu.make_async_copy(
                slots.at[panel_slot[k * blocks + window[w]], :, :, pl.ds(n * lanes, lanes)],
                panels.at[n, :, k * windows + w],
                came.at[n, k * windows + w],
            )
            for k in range(summed)
            for w in range(windows)
        ]
        for n in range(chunks)
    ]
    early = [
        pltpu.make_async_copy(source, target, first_came.at[n])
        for n, (source, target) in enumerate(
            ((tiles_in, tiles), (row_energy, row_part), (col_energy, col_part))
        )
    ]
    for fetch in early + sum(fetches, []):
        fetch.start()
    for fetch in early:
        fetch.wait()
    build_rows(mask, window, row_tile, tiles, rows, lhs)
    stores = []
    for n in range(chunks):
        for fetch in fetches[n]:
            fetch.wait()
        for first in range(0, lanes, MXU):
            for j in range(cols):
                term = jnp.dot(
                    lhs[...],
                    panels[n, j, :, :, pl.ds(first, MXU)].reshape(depth, MXU),
                    preferred_element_type=jnp.float32,
                )
                for part in range(MXU // LANES):
                    at = first + part * LANES
                    gap = row_part[...] + col_part[pl.ds(j, 1), pl.ds(n * lanes + at, LANES)]
                    guess = pl.reciprocal(gap, approx=True)
                    pairs[at // LANES, pl.ds(j, row_count, stride=cols), :] = term[
                        :, part * LANES : (part + 1) * LANES
                    ] * (guess * (2.0 - gap * guess))
        flat = done.at[n].reshape(row_count * cols, lanes)
        for part in range(lanes // LANES):
            flat[:, pl.ds(part * LANES, LANES)] = pairs[part].astype(out.dtype)
        stores.append(
            pltpu.make_async_copy(done.at[n], out.at[:, :, pl.ds(n * lanes, lanes)], left.at[n])
        )
        stores[-1].start()
    for store in stores:
        store.wait()


def contract(panel_slot, window, tile_mask, row_tile, tiles, row_energy, col_energy, slots, lanes):
    x_count, windows, occ_rows, c_local, tile_lanes = tiles.shape
    _, cols, width, width_virt = slots.shape
    summed = tile_mask.shape[1]
    half, count, chunks = tile_lanes // summed, summed * windows, width_virt // lanes
    row_count, depth = half * occ_rows, count * width
    smem = pl.BlockSpec(memory_space=pltpu.SMEM)
    hbm = pl.BlockSpec(memory_space=pltpu.HBM)
    return pl.pallas_call(
        contract_kernel,
        out_shape=jax.ShapeDtypeStruct((row_count, cols, width_virt), jnp.bfloat16),
        in_specs=[smem] * 4 + [hbm] * 4,
        out_specs=hbm,
        scratch_shapes=[
            pltpu.VMEM(tiles.shape, tiles.dtype),
            pltpu.VMEM(row_energy.shape, row_energy.dtype),
            pltpu.VMEM(col_energy.shape, col_energy.dtype),
            pltpu.VMEM((chunks, cols, count, width, lanes), jnp.bfloat16),
            pltpu.VMEM((half, occ_rows, depth), jnp.float32),
            pltpu.VMEM((row_count, depth), jnp.bfloat16),
            pltpu.VMEM((lanes // LANES, row_count * cols, LANES), jnp.float32),
            pltpu.VMEM((chunks, row_count, cols, lanes), jnp.bfloat16),
            pltpu.SemaphoreType.DMA((3,)),
            pltpu.SemaphoreType.DMA((chunks, count)),
            pltpu.SemaphoreType.DMA((chunks,)),
        ],
        compiler_params=pltpu.CompilerParams(vmem_limit_bytes=56 * MIB),
    )(
        panel_slot,
        window,
        tile_mask.reshape(occ_rows * summed, *tile_mask.shape[2:]),
        row_tile,
        tiles,
        row_energy,
        col_energy,
        slots,
    )


def body(
    amplitudes,
    cycle_panels,
    tile_mask,
    panel_slot,
    window_blocks,
    virt_energy,
    row_energy,
    col_energy,
):
    _, _, col_local, width_virt = cycle_panels.shape
    c_local = amplitudes.shape[2]
    occ_rows, occ_summed = tile_mask.shape[:2]
    perm_count = lax.axis_size("perm")
    a_local = amplitudes.shape[1] // perm_count
    p = lax.axis_index("perm")

    slots = lax.all_gather(jnp.swapaxes(cycle_panels[0], 0, 1), "perm", axis=0)

    blocks = jnp.swapaxes(amplitudes[0].T.reshape(c_local, perm_count, a_local), 0, 1)
    blocks = lax.all_to_all(blocks, "perm", 0, 0, tiled=True)
    blocks, virt_energy, row_energy = lax.optimization_barrier((blocks, virt_energy, row_energy))
    blocks = blocks.reshape(occ_rows, occ_summed, c_local, a_local)
    blocks = jnp.concatenate([blocks[:, k] for k in range(occ_summed)], axis=-1)
    row_virt = lax.dynamic_slice_in_dim(virt_energy, p * a_local, a_local)
    rows = row_virt[:, None] - row_energy[None, :]
    rows = jnp.broadcast_to(rows[..., None], (*rows.shape, LANES)).reshape(-1, LANES)
    columns = virt_energy[None, :] - col_energy[:, None]
    tiles = gather_by_exchange(blocks, ALONG_Z)
    tiles, rows, columns = lax.optimization_barrier((tiles, rows, columns))
    tiles = jnp.stack(
        [lax.dynamic_index_in_dim(tiles, window_blocks[w], 0, False) for w in range(window_blocks.shape[0])]
    )
    tiles = gather_by_exchange(tiles, ALONG_X)
    result = contract(
        panel_slot, window_blocks, tile_mask, (p >> 1).reshape(1), tiles, rows, columns, slots, 512
    )
    return result.reshape(a_local, occ_rows, col_local, width_virt)


def solution(mesh):
    in_specs = (
        P("perm", None, "summa"),
        P("perm", None, "summa", None),
        P(),
        P(),
        P(),
        P(),
        P(),
        P("summa"),
    )
    out_specs = P("perm", None, "summa", None)
    return jax.shard_map(body, mesh=mesh, in_specs=in_specs, out_specs=out_specs, check_vma=False)
```

```python
import jax
import jax.numpy as jnp
from jax import lax
from jax.experimental import pallas as pl
from jax.experimental.pallas import tpu as pltpu
from jax.sharding import PartitionSpec as P

CHIPS_Z, CHIPS_X = 8, 4
ALONG_Z = [[z * CHIPS_X + x for z in range(CHIPS_Z)] for x in range(CHIPS_X)]
ALONG_X = [[z * CHIPS_X + x for x in range(CHIPS_X)] for z in range(CHIPS_Z)]
MIB = 1024 * 1024
LANES, MXU = 128, 256


def gather_by_exchange(value, groups):
    count = len(groups[0])
    copies = jnp.broadcast_to(value[None], (count, *value.shape))
    return lax.all_to_all(copies, "summa", 0, 0, axis_index_groups=groups, tiled=True)


def rows_kernel(mask, window, row_tile, tiles, out, rows):
    x_count, windows, occ_rows, c_local, lanes = tiles.shape
    half, width = rows.shape[0], x_count * c_local
    summed = lanes // half
    for i in range(occ_rows):
        for w in range(windows):
            tile = tiles[:, w, i].reshape(width, lanes).astype(jnp.float32).T
            for k in range(summed):
                keep = mask[i * summed + k, row_tile[0], window[w]].astype(jnp.float32)
                rows[:, i, pl.ds((k * windows + w) * width, width)] = (
                    tile[k * half : (k + 1) * half] * keep
                )
    out[...] = rows[...].reshape(out.shape).astype(out.dtype)


def amplitude_rows(tile_mask, window, row_tile, tiles):
    x_count, windows, occ_rows, c_local, lanes = tiles.shape
    summed = tile_mask.shape[1]
    half, depth = lanes // summed, summed * windows * x_count * c_local
    smem = pl.BlockSpec(memory_space=pltpu.SMEM)
    return pl.pallas_call(
        rows_kernel,
        out_shape=jax.ShapeDtypeStruct((half * occ_rows, depth), jnp.bfloat16),
        in_specs=[smem, smem, smem, pl.BlockSpec(memory_space=pltpu.VMEM)],
        out_specs=pl.BlockSpec(memory_space=pltpu.VMEM),
        scratch_shapes=[
            pltpu.VMEM((half, occ_rows, depth), jnp.float32),
        ],
        compiler_params=pltpu.CompilerParams(vmem_limit_bytes=16 * MIB),
    )(tile_mask.reshape(occ_rows * summed, *tile_mask.shape[2:]), window, row_tile, tiles)


def contract_kernel(
    panel_slot, window, lhs, row_energy, col_energy, slots, out, panels, pairs, done, came, left
):
    row_count, depth = lhs.shape
    count, cols, width, width_virt = panels.shape
    windows = window.shape[0]
    summed = count // windows
    blocks = panel_slot.shape[0] // summed
    moves = []
    for k in range(summed):
        for w in range(windows):
            slot = panel_slot[k * blocks + window[w]]
            moves.append((slots.at[slot], panels.at[k * windows + w]))
    fetches = [pltpu.make_async_copy(*move, came.at[n]) for n, move in enumerate(moves)]
    for fetch in fetches:
        fetch.start()
    for fetch in fetches:
        fetch.wait()
    stores = []
    for n in range(done.shape[0]):
        for j in range(cols):
            term = jnp.dot(
                lhs[...],
                panels[:, j, :, pl.ds(n * MXU, MXU)].reshape(depth, MXU),
                preferred_element_type=jnp.float32,
            )
            for part in range(MXU // LANES):
                gap = row_energy[...] + col_energy[pl.ds(j, 1), pl.ds(n * MXU + part * LANES, LANES)]
                guess = pl.reciprocal(gap, approx=True)
                pairs[n, part, pl.ds(j, row_count, stride=cols), :] = term[
                    :, part * LANES : (part + 1) * LANES
                ] * (guess * (2.0 - gap * guess))
        flat = done.at[n].reshape(row_count * cols, MXU)
        for part in range(MXU // LANES):
            flat[:, pl.ds(part * LANES, LANES)] = pairs[n, part].astype(out.dtype)
        stores.append(
            pltpu.make_async_copy(done.at[n], out.at[:, :, pl.ds(n * MXU, MXU)], left.at[n])
        )
        stores[-1].start()
    for store in stores:
        store.wait()


def contract(panel_slot, window, lhs, row_energy, col_energy, slots):
    row_count, depth = lhs.shape
    _, cols, width, width_virt = slots.shape
    count, chunks = depth // width, width_virt // MXU
    smem, vmem = pl.BlockSpec(memory_space=pltpu.SMEM), pl.BlockSpec(memory_space=pltpu.VMEM)
    hbm = pl.BlockSpec(memory_space=pltpu.HBM)
    return pl.pallas_call(
        contract_kernel,
        out_shape=jax.ShapeDtypeStruct((row_count, cols, width_virt), jnp.bfloat16),
        in_specs=[smem] * 2 + [vmem] * 3 + [hbm],
        out_specs=hbm,
        scratch_shapes=[
            pltpu.VMEM((count, *slots.shape[1:]), slots.dtype),
            pltpu.VMEM((chunks, MXU // LANES, row_count * cols, LANES), jnp.float32),
            pltpu.VMEM((chunks, row_count, cols, MXU), jnp.bfloat16),
            pltpu.SemaphoreType.DMA((count,)),
            pltpu.SemaphoreType.DMA((chunks,)),
        ],
        compiler_params=pltpu.CompilerParams(vmem_limit_bytes=24 * MIB),
    )(
        panel_slot,
        window,
        lhs,
        row_energy,
        col_energy,
        pltpu.with_memory_space_constraint(slots, pltpu.HBM),
    )


def body(
    amplitudes,
    cycle_panels,
    tile_mask,
    panel_slot,
    window_blocks,
    virt_energy,
    row_energy,
    col_energy,
):
    _, _, col_local, width_virt = cycle_panels.shape
    c_local = amplitudes.shape[2]
    occ_rows, occ_summed = tile_mask.shape[:2]
    perm_count = lax.axis_size("perm")
    a_local = amplitudes.shape[1] // perm_count
    p = lax.axis_index("perm")

    slots = lax.all_gather(jnp.swapaxes(cycle_panels[0], 0, 1), "perm", axis=0)

    blocks = jnp.swapaxes(amplitudes[0].T.reshape(c_local, perm_count, a_local), 0, 1)
    blocks = lax.all_to_all(blocks, "perm", 0, 0, tiled=True)
    blocks, virt_energy, row_energy = lax.optimization_barrier((blocks, virt_energy, row_energy))
    blocks = blocks.reshape(occ_rows, occ_summed, c_local, a_local)
    blocks = jnp.concatenate([blocks[:, k] for k in range(occ_summed)], axis=-1)
    row_virt = lax.dynamic_slice_in_dim(virt_energy, p * a_local, a_local)
    rows = row_virt[:, None] - row_energy[None, :]
    rows = jnp.broadcast_to(rows[..., None], (*rows.shape, LANES)).reshape(-1, LANES)
    columns = virt_energy[None, :] - col_energy[:, None]
    tiles = gather_by_exchange(blocks, ALONG_Z)
    tiles = jnp.stack(
        [lax.dynamic_index_in_dim(tiles, window_blocks[w], 0, False) for w in range(window_blocks.shape[0])]
    )
    tiles = gather_by_exchange(tiles, ALONG_X)
    tiles, rows, columns = lax.optimization_barrier((tiles, rows, columns))
    lhs = amplitude_rows(tile_mask, window_blocks, (p >> 1).reshape(1), tiles)
    result = contract(panel_slot, window_blocks, lhs, rows, columns, slots)
    return result.reshape(a_local, occ_rows, col_local, width_virt)


def solution(mesh):
    in_specs = (
        P("perm", None, "summa"),
        P("perm", None, "summa", None),
        P(),
        P(),
        P(),
        P(),
        P(),
        P("summa"),
    )
    out_specs = P("perm", None, "summa", None)
    return jax.shard_map(body, mesh=mesh, in_specs=in_specs, out_specs=out_specs, check_vma=False)
```

```python
import jax
import jax.numpy as jnp
from jax import lax
from jax.experimental import pallas as pl
from jax.experimental.pallas import tpu as pltpu
from jax.sharding import PartitionSpec as P

CORES, CHIPS_Z, CHIPS_X = 2, 8, 4
ALONG_Z = [[z * CHIPS_X + x for z in range(CHIPS_Z)] for x in range(CHIPS_X)]
ALONG_X = [[z * CHIPS_X + x for x in range(CHIPS_X)] for z in range(CHIPS_Z)]
MIB = 1024 * 1024
LANES, MXU = 128, 256


def gather_by_exchange(value, groups):
    count = len(groups[0])
    copies = jnp.broadcast_to(value[None], (count, *value.shape))
    return lax.all_to_all(copies, "summa", 0, 0, axis_index_groups=groups, tiled=True)


def interleave(pairs, count):
    to = lax.broadcasted_iota(jnp.int32, (pairs * count, pairs * count), 0)
    of = lax.broadcasted_iota(jnp.int32, (pairs * count, pairs * count), 1)
    return (of == (to % pairs) * count + to // pairs).astype(jnp.float32).astype(jnp.bfloat16)


def split_kernel(panel, out):
    width, cols, width_virt = panel.shape
    order = interleave(width, cols)
    mixed = panel.reshape(width * cols, width_virt)
    for first in range(0, width_virt, MXU):
        apart = jnp.dot(order, mixed[:, pl.ds(first, MXU)], preferred_element_type=jnp.float32)
        out[:, :, pl.ds(first, MXU)] = apart.reshape(cols, width, MXU).astype(out.dtype)


def split_columns(panel):
    width, cols, width_virt = panel.shape
    vmem = pl.BlockSpec(memory_space=pltpu.VMEM)
    return pl.pallas_call(
        split_kernel,
        out_shape=jax.ShapeDtypeStruct((cols, width, width_virt), panel.dtype),
        in_specs=[vmem],
        out_specs=vmem,
        compiler_params=pltpu.CompilerParams(vmem_limit_bytes=16 * MIB),
    )(panel)


def rows_kernel(mask, window, row_tile, tiles, out, rows):
    x_count, windows, occ_rows, c_local, lanes = tiles.shape
    half, width = rows.shape[0], x_count * c_local
    summed = lanes // half
    blocks = lax.axis_size("perm") // CORES
    for i in range(occ_rows):
        for w in range(windows):
            tile = tiles[:, w, i].reshape(width, lanes).astype(jnp.float32).T
            for k in range(summed):
                keep = mask[((i * summed + k) * blocks + row_tile[0]) * blocks + window[w]].astype(
                    jnp.float32
                )
                rows[:, i, pl.ds((k * windows + w) * width, width)] = (
                    tile[k * half : (k + 1) * half] * keep
                )
    out[...] = rows[...].reshape(out.shape).astype(out.dtype)


def amplitude_rows(tile_mask, window, row_tile, tiles):
    x_count, windows, occ_rows, c_local, lanes = tiles.shape
    summed = tile_mask.shape[1]
    half, depth = lanes // summed, summed * windows * x_count * c_local
    smem = pl.BlockSpec(memory_space=pltpu.SMEM)
    return pl.pallas_call(
        rows_kernel,
        out_shape=jax.ShapeDtypeStruct((half * occ_rows, depth), jnp.bfloat16),
        in_specs=[smem, smem, smem, pl.BlockSpec(memory_space=pltpu.VMEM)],
        out_specs=pl.BlockSpec(memory_space=pltpu.VMEM),
        scratch_shapes=[
            pltpu.VMEM((half, occ_rows, depth), jnp.float32),
        ],
        compiler_params=pltpu.CompilerParams(vmem_limit_bytes=16 * MIB),
    )(tile_mask.reshape(-1), window, row_tile, tiles)


def contract_kernel(
    panel_slot, window, lhs, row_energy, col_energy, slots, out, panels, done, came, left
):
    row_count, depth = lhs.shape
    halves, count, cols, width, lanes = panels.shape
    windows = window.shape[0]
    summed = count // windows
    blocks = panel_slot.shape[0] // summed
    fetches = [
        [
            pltpu.make_async_copy(
                slots.at[panel_slot[k * blocks + window[w]], :, :, pl.ds(n * lanes, lanes)],
                panels.at[n, k * windows + w],
                came.at[n, k * windows + w],
            )
            for k in range(summed)
            for w in range(windows)
        ]
        for n in range(halves)
    ]
    for fetch in sum(fetches, []):
        fetch.start()
    together = MXU // cols
    order = interleave(cols, together)
    stores = []
    for n in range(halves):
        for fetch in fetches[n]:
            fetch.wait()
        for first in range(0, lanes, MXU):
            here = n * lanes + first
            rounded = []
            for j in range(cols):
                term = jnp.dot(
                    lhs[...],
                    panels[n, :, j, :, pl.ds(first, MXU)].reshape(depth, MXU),
                    preferred_element_type=jnp.float32,
                )
                parts = []
                for part in range(MXU // LANES):
                    gap = row_energy[...] + col_energy[pl.ds(j, 1), pl.ds(here + part * LANES, LANES)]
                    guess = pl.reciprocal(gap, approx=True)
                    parts.append(
                        term[:, part * LANES : (part + 1) * LANES] * (guess * (2.0 - gap * guess))
                    )
                rounded.append(jnp.concatenate(parts, axis=1).astype(out.dtype))
            for m in range(0, row_count, together):
                apart = jnp.concatenate([value[m : m + together] for value in rounded], axis=0)
                mixed = jnp.dot(order, apart, preferred_element_type=jnp.float32).astype(out.dtype)
                for part in range(MXU // LANES):
                    flat = done.at[here // LANES + part].reshape(row_count * cols, LANES)
                    flat[pl.ds(m * cols, MXU), :] = mixed[:, part * LANES : (part + 1) * LANES]
            for part in range(here // LANES, here // LANES + MXU // LANES):
                stores.append(
                    pltpu.make_async_copy(
                        done.at[part], out.at[:, :, pl.ds(part * LANES, LANES)], left.at[part]
                    )
                )
                stores[-1].start()
    for store in stores:
        store.wait()


def contract(panel_slot, window, lhs, row_energy, col_energy, slots):
    row_count, depth = lhs.shape
    _, cols, width, width_virt = slots.shape
    count, parts, halves = depth // width, width_virt // LANES, 2
    smem, vmem = pl.BlockSpec(memory_space=pltpu.SMEM), pl.BlockSpec(memory_space=pltpu.VMEM)
    hbm = pl.BlockSpec(memory_space=pltpu.HBM)
    return pl.pallas_call(
        contract_kernel,
        out_shape=jax.ShapeDtypeStruct((row_count, cols, width_virt), jnp.bfloat16),
        in_specs=[smem] * 2 + [vmem] * 3 + [hbm],
        out_specs=hbm,
        scratch_shapes=[
            pltpu.VMEM((halves, count, cols, width, width_virt // halves), slots.dtype),
            pltpu.VMEM((parts, row_count, cols, LANES), jnp.bfloat16),
            pltpu.SemaphoreType.DMA((halves, count)),
            pltpu.SemaphoreType.DMA((parts,)),
        ],
        compiler_params=pltpu.CompilerParams(vmem_limit_bytes=24 * MIB),
    )(
        panel_slot,
        window,
        lhs,
        row_energy,
        col_energy,
        pltpu.with_memory_space_constraint(slots, pltpu.HBM),
    )


def body(
    amplitudes,
    cycle_panels,
    tile_mask,
    panel_slot,
    window_blocks,
    virt_energy,
    row_energy,
    col_energy,
):
    _, _, col_local, width_virt = cycle_panels.shape
    c_local = amplitudes.shape[2]
    occ_rows, occ_summed = tile_mask.shape[:2]
    perm_count = lax.axis_size("perm")
    a_local = amplitudes.shape[1] // perm_count
    p = lax.axis_index("perm")

    slots = lax.all_gather(split_columns(cycle_panels[0]), "perm", axis=0)

    tile_width = CORES * a_local
    blocks = jnp.swapaxes(amplitudes[0].T.reshape(c_local, perm_count // CORES, tile_width), 0, 1)
    blocks = jnp.repeat(blocks, CORES, axis=0)
    blocks = lax.all_to_all(blocks, "perm", 0, 0, tiled=True)
    blocks, virt_energy, row_energy = lax.optimization_barrier((blocks, virt_energy, row_energy))
    blocks = blocks.reshape(occ_rows, occ_summed, c_local, tile_width)
    blocks = jnp.where(
        p & 1,
        jnp.concatenate([blocks[:, k, :, a_local:] for k in range(occ_summed)], axis=-1),
        jnp.concatenate([blocks[:, k, :, :a_local] for k in range(occ_summed)], axis=-1),
    )
    row_virt = lax.dynamic_slice_in_dim(virt_energy, p * a_local, a_local)
    rows = row_virt[:, None] - row_energy[None, :]
    rows = jnp.broadcast_to(rows[..., None], (*rows.shape, LANES)).reshape(-1, LANES)
    columns = virt_energy[None, :] - col_energy[:, None]
    tiles = gather_by_exchange(blocks, ALONG_Z)
    tiles = jnp.stack(
        [lax.dynamic_index_in_dim(tiles, window_blocks[w], 0, False) for w in range(window_blocks.shape[0])]
    )
    tiles = gather_by_exchange(tiles, ALONG_X)
    tiles, rows, columns = lax.optimization_barrier((tiles, rows, columns))
    lhs = amplitude_rows(tile_mask, window_blocks, (p >> 1).reshape(1), tiles)
    result = contract(panel_slot, window_blocks, lhs, rows, columns, slots)
    return result.reshape(a_local, occ_rows, col_local, width_virt)


def solution(mesh):
    in_specs = (
        P("perm", None, "summa"),
        P("perm", None, "summa", None),
        P(),
        P(),
        P(),
        P(),
        P(),
        P("summa"),
    )
    out_specs = P("perm", None, "summa", None)
    return jax.shard_map(body, mesh=mesh, in_specs=in_specs, out_specs=out_specs, check_vma=False)
```

```python
import jax
import jax.numpy as jnp
from jax import lax
from jax.experimental import pallas as pl
from jax.experimental.pallas import tpu as pltpu
from jax.sharding import PartitionSpec as P

CORES, CHIPS_Z, CHIPS_X = 2, 8, 4
ALONG_Z = [[z * CHIPS_X + x for z in range(CHIPS_Z)] for x in range(CHIPS_X)]
ALONG_X = [[z * CHIPS_X + x for x in range(CHIPS_X)] for z in range(CHIPS_Z)]
MIB = 1024 * 1024
LANES, MXU = 128, 256


def gather_by_exchange(value, groups):
    count = len(groups[0])
    copies = jnp.broadcast_to(value[None], (count, *value.shape))
    return lax.all_to_all(copies, "summa", 0, 0, axis_index_groups=groups, tiled=True)


def interleave(pairs, count):
    to = lax.broadcasted_iota(jnp.int32, (pairs * count, pairs * count), 0)
    of = lax.broadcasted_iota(jnp.int32, (pairs * count, pairs * count), 1)
    return (of == (to % pairs) * count + to // pairs).astype(jnp.float32).astype(jnp.bfloat16)


def split_kernel(panel, out, mixed, apart, came, left):
    halves, width, cols, lanes = mixed.shape
    order = interleave(width, cols)
    fetches, stores = [], []
    for n in range(halves):
        here = pl.ds(n * lanes, lanes)
        fetches.append(pltpu.make_async_copy(panel.at[:, :, here], mixed.at[n], came.at[n]))
        stores.append(pltpu.make_async_copy(apart.at[n], out.at[:, :, here], left.at[n]))
        fetches[n].start()
    for n in range(halves):
        fetches[n].wait()
        rows = mixed.at[n].reshape(width * cols, lanes)
        for first in range(0, lanes, MXU):
            some = jnp.dot(order, rows[:, pl.ds(first, MXU)], preferred_element_type=jnp.float32)
            apart[n, :, :, pl.ds(first, MXU)] = some.reshape(cols, width, MXU).astype(out.dtype)
        stores[n].start()
    for store in stores:
        store.wait()


def split_columns(panel):
    width, cols, width_virt = panel.shape
    halves, hbm = 2, pl.BlockSpec(memory_space=pltpu.HBM)
    return pl.pallas_call(
        split_kernel,
        out_shape=pltpu.HBM((cols, width, width_virt), panel.dtype),
        in_specs=[hbm],
        out_specs=hbm,
        scratch_shapes=[
            pltpu.VMEM((halves, width, cols, width_virt // halves), panel.dtype),
            pltpu.VMEM((halves, cols, width, width_virt // halves), panel.dtype),
            pltpu.SemaphoreType.DMA((halves,)),
            pltpu.SemaphoreType.DMA((halves,)),
        ],
        compiler_params=pltpu.CompilerParams(vmem_limit_bytes=16 * MIB),
    )(pltpu.with_memory_space_constraint(panel, pltpu.HBM))


def along_x(value, step):
    pairs = [(group[x], group[(x + step) % CHIPS_X]) for group in ALONG_X for x in range(CHIPS_X)]
    return lax.ppermute(value, "summa", pairs)


def rows_kernel(mask, window, place, own, left, right, far_low, far_high, out, tiles, rows):
    windows, occ_rows, c_local, lanes = own.shape
    x_count, half = tiles.shape[0], rows.shape[0]
    width, summed = x_count * c_local, lanes // half
    blocks = lax.axis_size("perm") // CORES
    row_tile, x = place[0], place[1]
    far = (x + 2) & (x_count - 1)
    low = far_low.shape[0]
    tiles[x] = own[...]
    tiles[(x - 1) & (x_count - 1)] = left[...]
    tiles[(x + 1) & (x_count - 1)] = right[...]
    tiles[far, pl.ds(0, low)] = far_low[...]
    tiles[far, pl.ds(low, windows - low)] = far_high[...]
    for i in range(occ_rows):
        for w in range(windows):
            tile = tiles[:, w, i].reshape(width, lanes).astype(jnp.float32).T
            for k in range(summed):
                keep = mask[((i * summed + k) * blocks + row_tile) * blocks + window[w]]
                rows[:, i, pl.ds((k * windows + w) * width, width)] = (
                    tile[k * half : (k + 1) * half] * keep.astype(jnp.float32)
                )
    out[...] = rows[...].reshape(out.shape).astype(out.dtype)


def amplitude_rows(tile_mask, window, place, parts):
    windows, occ_rows, c_local, lanes = parts[0].shape
    summed = tile_mask.shape[1]
    half, depth = lanes // summed, summed * windows * CHIPS_X * c_local
    smem, vmem = pl.BlockSpec(memory_space=pltpu.SMEM), pl.BlockSpec(memory_space=pltpu.VMEM)
    return pl.pallas_call(
        rows_kernel,
        out_shape=jax.ShapeDtypeStruct((half * occ_rows, depth), jnp.bfloat16),
        in_specs=[smem, smem, smem] + [vmem] * len(parts),
        out_specs=vmem,
        scratch_shapes=[
            pltpu.VMEM((CHIPS_X, *parts[0].shape), parts[0].dtype),
            pltpu.VMEM((half, occ_rows, depth), jnp.float32),
        ],
        compiler_params=pltpu.CompilerParams(vmem_limit_bytes=16 * MIB),
    )(tile_mask.reshape(-1), window, place, *parts)


def contract_kernel(
    panel_slot, window, lhs, inverse, slots, out, panels, done, came, left
):
    row_count, depth = lhs.shape
    halves, count, cols, width, lanes = panels.shape
    windows = window.shape[0]
    summed = count // windows
    blocks = panel_slot.shape[0] // summed
    fetches = [
        [
            pltpu.make_async_copy(
                slots.at[panel_slot[k * blocks + window[w]], :, :, pl.ds(n * lanes, lanes)],
                panels.at[n, k * windows + w],
                came.at[n, k * windows + w],
            )
            for k in range(summed)
            for w in range(windows)
        ]
        for n in range(halves)
    ]
    for fetch in sum(fetches, []):
        fetch.start()
    together = MXU // cols
    order = interleave(cols, together)
    stores = []
    for n in range(halves):
        for fetch in fetches[n]:
            fetch.wait()
        for first in range(0, lanes, MXU):
            here = n * lanes + first
            rounded = []
            for j in range(cols):
                term = jnp.dot(
                    lhs[...],
                    panels[n, :, j, :, pl.ds(first, MXU)].reshape(depth, MXU),
                    preferred_element_type=jnp.float32,
                )
                term = term * inverse[j, :, pl.ds(here, MXU)]
                rounded.append(term.astype(out.dtype))
            for m in range(0, row_count, together):
                apart = jnp.concatenate([value[m : m + together] for value in rounded], axis=0)
                mixed = jnp.dot(order, apart, preferred_element_type=jnp.float32).astype(out.dtype)
                for part in range(MXU // LANES):
                    flat = done.at[here // LANES + part].reshape(row_count * cols, LANES)
                    flat[pl.ds(m * cols, MXU), :] = mixed[:, part * LANES : (part + 1) * LANES]
            for part in range(here // LANES, here // LANES + MXU // LANES):
                stores.append(
                    pltpu.make_async_copy(
                        done.at[part], out.at[:, :, pl.ds(part * LANES, LANES)], left.at[part]
                    )
                )
                stores[-1].start()
    for store in stores:
        store.wait()


def contract(panel_slot, window, lhs, inverse, slots):
    row_count, depth = lhs.shape
    _, cols, width, width_virt = slots.shape
    count, parts, halves = depth // width, width_virt // LANES, width_virt // MXU
    smem, vmem = pl.BlockSpec(memory_space=pltpu.SMEM), pl.BlockSpec(memory_space=pltpu.VMEM)
    hbm = pl.BlockSpec(memory_space=pltpu.HBM)
    return pl.pallas_call(
        contract_kernel,
        out_shape=jax.ShapeDtypeStruct((row_count, cols, width_virt), jnp.bfloat16),
        in_specs=[smem] * 2 + [vmem] * 2 + [hbm],
        out_specs=hbm,
        scratch_shapes=[
            pltpu.VMEM((halves, count, cols, width, width_virt // halves), slots.dtype),
            pltpu.VMEM((parts, row_count, cols, LANES), jnp.bfloat16),
            pltpu.SemaphoreType.DMA((halves, count)),
            pltpu.SemaphoreType.DMA((parts,)),
        ],
        compiler_params=pltpu.CompilerParams(vmem_limit_bytes=24 * MIB),
    )(
        panel_slot,
        window,
        lhs,
        inverse,
        pltpu.with_memory_space_constraint(slots, pltpu.HBM),
    )


def body(
    amplitudes,
    cycle_panels,
    tile_mask,
    panel_slot,
    window_blocks,
    virt_energy,
    row_energy,
    col_energy,
):
    _, _, col_local, width_virt = cycle_panels.shape
    c_local = amplitudes.shape[2]
    occ_rows, occ_summed = tile_mask.shape[:2]
    perm_count = lax.axis_size("perm")
    a_local = amplitudes.shape[1] // perm_count
    p = lax.axis_index("perm")

    slots = lax.all_gather(split_columns(cycle_panels[0]), "perm", axis=0)

    blocks = jnp.swapaxes(amplitudes[0].T.reshape(c_local, perm_count, a_local), 0, 1)
    blocks = lax.all_to_all(blocks, "perm", 0, 0, tiled=True)
    blocks, virt_energy, row_energy = lax.optimization_barrier((blocks, virt_energy, row_energy))
    blocks = blocks.reshape(occ_rows, occ_summed, c_local, a_local)
    blocks = jnp.concatenate([blocks[:, k] for k in range(occ_summed)], axis=-1)
    row_virt = lax.dynamic_slice_in_dim(virt_energy, p * a_local, a_local)
    rows = (row_virt[:, None] - row_energy[None, :]).reshape(1, -1, 1)
    columns = virt_energy[None, :] - col_energy[:, None]
    tiles = gather_by_exchange(blocks, ALONG_Z)
    tiles = jnp.stack(
        [lax.dynamic_index_in_dim(tiles, window_blocks[w], 0, False) for w in range(window_blocks.shape[0])]
    )
    left, right = along_x(tiles, 1), along_x(tiles, -1)
    low = tiles.shape[0] // 2
    parts = (tiles, left, right, along_x(left[:low], 1), along_x(right[low:], -1))
    inverse = 1.0 / (rows + columns[:, None, :])
    *parts, inverse = lax.optimization_barrier((*parts, inverse))
    place = jnp.stack([p >> 1, lax.axis_index("summa") & (CHIPS_X - 1)])
    lhs = amplitude_rows(tile_mask, window_blocks, place, parts)
    result = contract(panel_slot, window_blocks, lhs, inverse, slots)
    return result.reshape(a_local, occ_rows, col_local, width_virt)


def solution(mesh):
    in_specs = (
        P("perm", None, "summa"),
        P("perm", None, "summa", None),
        P(),
        P(),
        P(),
        P(),
        P(),
        P("summa"),
    )
    out_specs = P("perm", None, "summa", None)
    return jax.shard_map(body, mesh=mesh, in_specs=in_specs, out_specs=out_specs, check_vma=False)
```

```python
import jax
import jax.numpy as jnp
from jax import lax
from jax.experimental import pallas as pl
from jax.experimental.pallas import tpu as pltpu
from jax.sharding import PartitionSpec as P

CORES, CHIPS_Z, CHIPS_X = 2, 8, 4
ALONG_Z = [[z * CHIPS_X + x for z in range(CHIPS_Z)] for x in range(CHIPS_X)]
ALONG_X = [[z * CHIPS_X + x for x in range(CHIPS_X)] for z in range(CHIPS_Z)]
MIB = 1024 * 1024
LANES, MXU = 128, 256


def gather_by_exchange(value, groups):
    count = len(groups[0])
    copies = jnp.broadcast_to(value[None], (count, *value.shape))
    return lax.all_to_all(copies, "summa", 0, 0, axis_index_groups=groups, tiled=True)


def interleave(pairs, count):
    to = lax.broadcasted_iota(jnp.int32, (pairs * count, pairs * count), 0)
    of = lax.broadcasted_iota(jnp.int32, (pairs * count, pairs * count), 1)
    return (of == (to % pairs) * count + to // pairs).astype(jnp.float32).astype(jnp.bfloat16)


def fetch_kernel(panel_slot, window, slots, out, mixed, came):
    count, cols, width, width_virt = out.shape
    windows = window.shape[0]
    blocks = panel_slot.shape[0] * windows // count
    fetches = []
    for m in range(count):
        slot = panel_slot[m // windows * blocks + window[m % windows]]
        fetches.append(pltpu.make_async_copy(slots.at[slot], mixed.at[m], came.at[m]))
        fetches[m].start()
    parts = width_virt // LANES
    some = MXU // (parts * cols)
    to = lax.broadcasted_iota(jnp.int32, (MXU, MXU), 0)
    of = lax.broadcasted_iota(jnp.int32, (MXU, MXU), 1)
    part, j, c = to // (cols * some), to // some % cols, to % some
    order = (of == (c * parts + part) * cols + j).astype(jnp.float32).astype(out.dtype)
    beside = MXU // LANES
    for m in range(count):
        fetches[m].wait()
        for first in range(0, width, some * beside):
            rows = [
                mixed[m, pl.ds((first + n * some) * parts * cols, MXU), :] for n in range(beside)
            ]
            apart = jnp.dot(
                order, jnp.concatenate(rows, axis=1), preferred_element_type=jnp.float32
            ).astype(out.dtype)
            for n in range(beside):
                for part in range(parts):
                    for j in range(cols):
                        out[m, j, pl.ds(first + n * some, some), pl.ds(part * LANES, LANES)] = apart[
                            (part * cols + j) * some : (part * cols + j + 1) * some,
                            n * LANES : (n + 1) * LANES,
                        ]


def fetch(panel_slot, window, slots, summed, cols, width):
    count = summed * window.shape[0]
    width_virt = slots.shape[1] // (cols * width) * LANES
    smem = pl.BlockSpec(memory_space=pltpu.SMEM)
    return pl.pallas_call(
        fetch_kernel,
        out_shape=pltpu.VMEM((count, cols, width, width_virt), slots.dtype),
        in_specs=[smem, smem, pl.BlockSpec(memory_space=pltpu.HBM)],
        out_specs=pl.BlockSpec(memory_space=pltpu.VMEM),
        scratch_shapes=[
            pltpu.VMEM((count, *slots.shape[1:]), slots.dtype),
            pltpu.SemaphoreType.DMA((count,)),
        ],
        compiler_params=pltpu.CompilerParams(vmem_limit_bytes=16 * MIB),
    )(panel_slot, window, pltpu.with_memory_space_constraint(slots, pltpu.HBM))


def rows_kernel(mask, window, row_tile, tiles, out, rows):
    x_count, windows, occ_rows, c_local, lanes = tiles.shape
    half, width = rows.shape[0], x_count * c_local
    summed = lanes // half
    blocks = lax.axis_size("perm") // CORES
    for i in range(occ_rows):
        for w in range(windows):
            tile = tiles[:, w, i].reshape(width, lanes).astype(jnp.float32).T
            for k in range(summed):
                keep = mask[((i * summed + k) * blocks + row_tile[0]) * blocks + window[w]].astype(
                    jnp.float32
                )
                rows[:, i, pl.ds((k * windows + w) * width, width)] = (
                    tile[k * half : (k + 1) * half] * keep
                )
    out[...] = rows[...].reshape(out.shape).astype(out.dtype)


def amplitude_rows(tile_mask, window, row_tile, tiles):
    x_count, windows, occ_rows, c_local, lanes = tiles.shape
    summed = tile_mask.shape[1]
    half, depth = lanes // summed, summed * windows * x_count * c_local
    smem = pl.BlockSpec(memory_space=pltpu.SMEM)
    return pl.pallas_call(
        rows_kernel,
        out_shape=jax.ShapeDtypeStruct((half * occ_rows, depth), jnp.bfloat16),
        in_specs=[smem, smem, smem, pl.BlockSpec(memory_space=pltpu.VMEM)],
        out_specs=pl.BlockSpec(memory_space=pltpu.VMEM),
        scratch_shapes=[
            pltpu.VMEM((half, occ_rows, depth), jnp.float32),
        ],
        compiler_params=pltpu.CompilerParams(vmem_limit_bytes=16 * MIB),
    )(tile_mask.reshape(-1), window, row_tile, tiles)


def contract_kernel(lhs, row_energy, col_energy, panels, out, done, left):
    row_count, depth = lhs.shape
    _, cols, _, width_virt = panels.shape
    together = MXU // cols
    order = interleave(cols, together)
    stores = []
    for here in range(0, width_virt, MXU):
        rounded = []
        for j in range(cols):
            term = jnp.dot(
                lhs[...],
                panels[:, j, :, pl.ds(here, MXU)].reshape(depth, MXU),
                preferred_element_type=jnp.float32,
            )
            parts = []
            for part in range(MXU // LANES):
                gap = row_energy[...] + col_energy[pl.ds(j, 1), pl.ds(here + part * LANES, LANES)]
                guess = pl.reciprocal(gap, approx=True)
                parts.append(
                    term[:, part * LANES : (part + 1) * LANES] * (guess * (2.0 - gap * guess))
                )
            rounded.append(jnp.concatenate(parts, axis=1).astype(out.dtype))
        for m in range(0, row_count, together):
            apart = jnp.concatenate([value[m : m + together] for value in rounded], axis=0)
            mixed = jnp.dot(order, apart, preferred_element_type=jnp.float32).astype(out.dtype)
            for part in range(MXU // LANES):
                flat = done.at[here // LANES + part].reshape(row_count * cols, LANES)
                flat[pl.ds(m * cols, MXU), :] = mixed[:, part * LANES : (part + 1) * LANES]
        for part in range(here // LANES, here // LANES + MXU // LANES):
            stores.append(
                pltpu.make_async_copy(
                    done.at[part], out.at[:, :, pl.ds(part * LANES, LANES)], left.at[part]
                )
            )
            stores[-1].start()
    for store in stores:
        store.wait()


def contract(lhs, row_energy, col_energy, panels):
    row_count = lhs.shape[0]
    _, cols, _, width_virt = panels.shape
    parts = width_virt // LANES
    vmem = pl.BlockSpec(memory_space=pltpu.VMEM)
    return pl.pallas_call(
        contract_kernel,
        out_shape=jax.ShapeDtypeStruct((row_count, cols, width_virt), jnp.bfloat16),
        in_specs=[vmem] * 4,
        out_specs=pl.BlockSpec(memory_space=pltpu.HBM),
        scratch_shapes=[
            pltpu.VMEM((parts, row_count, cols, LANES), jnp.bfloat16),
            pltpu.SemaphoreType.DMA((parts,)),
        ],
        compiler_params=pltpu.CompilerParams(vmem_limit_bytes=16 * MIB),
    )(lhs, row_energy, col_energy, pltpu.with_memory_space_constraint(panels, pltpu.VMEM))


def body(
    amplitudes,
    cycle_panels,
    tile_mask,
    panel_slot,
    window_blocks,
    virt_energy,
    row_energy,
    col_energy,
):
    _, _, col_local, width_virt = cycle_panels.shape
    c_local = amplitudes.shape[2]
    occ_rows, occ_summed = tile_mask.shape[:2]
    perm_count = lax.axis_size("perm")
    a_local = amplitudes.shape[1] // perm_count
    p = lax.axis_index("perm")

    width = cycle_panels.shape[1]
    flat = cycle_panels.reshape(width, col_local, width_virt // LANES, LANES)
    flat = jnp.swapaxes(flat, 1, 2).reshape(-1, LANES)
    slots = lax.all_gather(flat, "perm", axis=0)

    blocks = jnp.swapaxes(amplitudes[0].T.reshape(c_local, perm_count, a_local), 0, 1)
    blocks = lax.all_to_all(blocks, "perm", 0, 0, tiled=True)
    blocks, virt_energy, row_energy = lax.optimization_barrier((blocks, virt_energy, row_energy))
    blocks = blocks.reshape(occ_rows, occ_summed, c_local, a_local)
    blocks = jnp.concatenate([blocks[:, k] for k in range(occ_summed)], axis=-1)
    row_virt = lax.dynamic_slice_in_dim(virt_energy, p * a_local, a_local)
    rows = row_virt[:, None] - row_energy[None, :]
    rows = jnp.broadcast_to(rows[..., None], (*rows.shape, LANES)).reshape(-1, LANES)
    columns = virt_energy[None, :] - col_energy[:, None]
    tiles = gather_by_exchange(blocks, ALONG_Z)
    tiles = jnp.stack(
        [lax.dynamic_index_in_dim(tiles, window_blocks[w], 0, False) for w in range(window_blocks.shape[0])]
    )
    tiles = gather_by_exchange(tiles, ALONG_X)
    panels = fetch(panel_slot, window_blocks, slots, occ_summed, col_local, width)
    tiles, rows, columns, panels = lax.optimization_barrier((tiles, rows, columns, panels))
    lhs = amplitude_rows(tile_mask, window_blocks, (p >> 1).reshape(1), tiles)
    result = contract(lhs, rows, columns, panels)
    return result.reshape(a_local, occ_rows, col_local, width_virt)


def solution(mesh):
    in_specs = (
        P("perm", None, "summa"),
        P("perm", None, "summa", None),
        P(),
        P(),
        P(),
        P(),
        P(),
        P("summa"),
    )
    out_specs = P("perm", None, "summa", None)
    return jax.shard_map(body, mesh=mesh, in_specs=in_specs, out_specs=out_specs, check_vma=False)
```

```python
import jax
import jax.numpy as jnp
from jax import lax
from jax.experimental import pallas as pl
from jax.experimental.pallas import tpu as pltpu
from jax.sharding import PartitionSpec as P

CORES, CHIPS_Z, CHIPS_X = 2, 8, 4
ALONG_Z = [[z * CHIPS_X + x for z in reversed(range(CHIPS_Z))] for x in range(CHIPS_X)]
ALONG_X = [[z * CHIPS_X + x for x in reversed(range(CHIPS_X))] for z in range(CHIPS_Z)]
MIB = 1024 * 1024
LANES, MXU = 128, 256


def gather_by_exchange(value, groups):
    count = len(groups[0])
    copies = jnp.broadcast_to(value[None], (count, *value.shape))
    return lax.all_to_all(copies, "summa", 0, 0, axis_index_groups=groups, tiled=True)


def interleave(pairs, count):
    to = lax.broadcasted_iota(jnp.int32, (pairs * count, pairs * count), 0)
    of = lax.broadcasted_iota(jnp.int32, (pairs * count, pairs * count), 1)
    return (of == (to % pairs) * count + to // pairs).astype(jnp.float32).astype(jnp.bfloat16)


def rows_kernel(mask, window, row_tile, tiles, out, rows):
    x_count, windows, occ_rows, c_local, lanes = tiles.shape
    half, width = rows.shape[0], x_count * c_local
    summed = lanes // half
    blocks = lax.axis_size("perm") // CORES
    for i in range(occ_rows):
        for w in range(windows):
            tile = jnp.concatenate([tiles[x, w, i] for x in reversed(range(x_count))], axis=0)
            tile = tile.astype(jnp.float32).T
            for k in range(summed):
                keep = mask[((i * summed + k) * blocks + row_tile[0]) * blocks + window[w]].astype(
                    jnp.float32
                )
                rows[:, i, pl.ds((k * windows + w) * width, width)] = (
                    tile[k * half : (k + 1) * half] * keep
                )
    out[...] = rows[...].reshape(out.shape).astype(out.dtype)


def amplitude_rows(tile_mask, window, row_tile, tiles):
    x_count, windows, occ_rows, c_local, lanes = tiles.shape
    summed = tile_mask.shape[1]
    half, depth = lanes // summed, summed * windows * x_count * c_local
    smem = pl.BlockSpec(memory_space=pltpu.SMEM)
    return pl.pallas_call(
        rows_kernel,
        out_shape=jax.ShapeDtypeStruct((half * occ_rows, depth), jnp.bfloat16),
        in_specs=[smem, smem, smem, pl.BlockSpec(memory_space=pltpu.VMEM)],
        out_specs=pl.BlockSpec(memory_space=pltpu.VMEM),
        scratch_shapes=[
            pltpu.VMEM((half, occ_rows, depth), jnp.float32),
        ],
        compiler_params=pltpu.CompilerParams(vmem_limit_bytes=16 * MIB),
    )(tile_mask.reshape(-1), window, row_tile, tiles)


def contract_kernel(
    panel_slot, window, lhs, row_energy, col_energy, slots, out, panels, done, came, left
):
    row_count, depth = lhs.shape
    halves, count, cols, width, lanes = panels.shape
    windows = window.shape[0]
    summed = count // windows
    blocks = panel_slot.shape[0] // summed
    fetches = [
        [
            pltpu.make_async_copy(
                slots.at[panel_slot[k * blocks + window[w]], :, :, pl.ds(n * lanes, lanes)],
                panels.at[n, k * windows + w],
                came.at[n, k * windows + w],
            )
            for k in range(summed)
            for w in range(windows)
        ]
        for n in range(halves)
    ]
    for fetch in sum(fetches, []):
        fetch.start()
    together = MXU // cols
    order = interleave(cols, together)
    stores = []
    for n in range(halves):
        for fetch in fetches[n]:
            fetch.wait()
        for first in range(0, lanes, MXU):
            here = n * lanes + first
            rounded = []
            for j in range(cols):
                term = jnp.dot(
                    lhs[...],
                    panels[n, :, j, :, pl.ds(first, MXU)].reshape(depth, MXU),
                    preferred_element_type=jnp.float32,
                )
                parts = []
                for part in range(MXU // LANES):
                    gap = row_energy[...] + col_energy[pl.ds(j, 1), pl.ds(here + part * LANES, LANES)]
                    guess = pl.reciprocal(gap, approx=True)
                    parts.append(
                        term[:, part * LANES : (part + 1) * LANES] * (guess * (2.0 - gap * guess))
                    )
                rounded.append(jnp.concatenate(parts, axis=1).astype(out.dtype))
            for m in range(0, row_count, together):
                apart = jnp.concatenate([value[m : m + together] for value in rounded], axis=0)
                mixed = jnp.dot(order, apart, preferred_element_type=jnp.float32).astype(out.dtype)
                for part in range(MXU // LANES):
                    flat = done.at[here // LANES + part].reshape(row_count * cols, LANES)
                    flat[pl.ds(m * cols, MXU), :] = mixed[:, part * LANES : (part + 1) * LANES]
            for part in range(here // LANES, here // LANES + MXU // LANES):
                stores.append(
                    pltpu.make_async_copy(
                        done.at[part], out.at[:, :, pl.ds(part * LANES, LANES)], left.at[part]
                    )
                )
                stores[-1].start()
    for store in stores:
        store.wait()


def contract(panel_slot, window, lhs, row_energy, col_energy, slots):
    row_count, depth = lhs.shape
    _, cols, width, width_virt = slots.shape
    count, parts, halves = depth // width, width_virt // LANES, 2
    smem, vmem = pl.BlockSpec(memory_space=pltpu.SMEM), pl.BlockSpec(memory_space=pltpu.VMEM)
    hbm = pl.BlockSpec(memory_space=pltpu.HBM)
    return pl.pallas_call(
        contract_kernel,
        out_shape=jax.ShapeDtypeStruct((row_count, cols, width_virt), jnp.bfloat16),
        in_specs=[smem] * 2 + [vmem] * 3 + [hbm],
        out_specs=hbm,
        scratch_shapes=[
            pltpu.VMEM((halves, count, cols, width, width_virt // halves), slots.dtype),
            pltpu.VMEM((parts, row_count, cols, LANES), jnp.bfloat16),
            pltpu.SemaphoreType.DMA((halves, count)),
            pltpu.SemaphoreType.DMA((parts,)),
        ],
        compiler_params=pltpu.CompilerParams(vmem_limit_bytes=24 * MIB),
    )(
        panel_slot,
        window,
        lhs,
        row_energy,
        col_energy,
        pltpu.with_memory_space_constraint(slots, pltpu.HBM),
    )


def body(
    amplitudes,
    cycle_panels,
    tile_mask,
    panel_slot,
    window_blocks,
    virt_energy,
    row_energy,
    col_energy,
):
    _, _, col_local, width_virt = cycle_panels.shape
    c_local = amplitudes.shape[2]
    occ_rows, occ_summed = tile_mask.shape[:2]
    perm_count = lax.axis_size("perm")
    a_local = amplitudes.shape[1] // perm_count
    p = lax.axis_index("perm")

    slots = lax.all_gather(jnp.swapaxes(cycle_panels[0], 0, 1), "perm", axis=0)

    blocks = jnp.swapaxes(amplitudes[0].T.reshape(c_local, perm_count, a_local), 0, 1)
    blocks = lax.all_to_all(blocks, "perm", 0, 0, tiled=True)
    blocks, virt_energy, row_energy = lax.optimization_barrier((blocks, virt_energy, row_energy))
    blocks = blocks.reshape(occ_rows, occ_summed, c_local, a_local)
    blocks = jnp.concatenate([blocks[:, k] for k in range(occ_summed)], axis=-1)
    row_virt = lax.dynamic_slice_in_dim(virt_energy, p * a_local, a_local)
    rows = row_virt[:, None] - row_energy[None, :]
    rows = jnp.broadcast_to(rows[..., None], (*rows.shape, LANES)).reshape(-1, LANES)
    columns = virt_energy[None, :] - col_energy[:, None]
    tiles = gather_by_exchange(blocks, ALONG_Z)
    tiles = jnp.stack(
        [lax.dynamic_index_in_dim(tiles, CHIPS_Z - 1 - window_blocks[w], 0, False) for w in range(window_blocks.shape[0])]
    )
    tiles = gather_by_exchange(tiles, ALONG_X)
    tiles, rows, columns = lax.optimization_barrier((tiles, rows, columns))
    lhs = amplitude_rows(tile_mask, window_blocks, (p >> 1).reshape(1), tiles)
    result = contract(panel_slot, window_blocks, lhs, rows, columns, slots)
    return result.reshape(a_local, occ_rows, col_local, width_virt)


def solution(mesh):
    in_specs = (
        P("perm", None, "summa"),
        P("perm", None, "summa", None),
        P(),
        P(),
        P(),
        P(),
        P(),
        P("summa"),
    )
    out_specs = P("perm", None, "summa", None)
    return jax.shard_map(body, mesh=mesh, in_specs=in_specs, out_specs=out_specs, check_vma=False)
```

```python
import jax
import jax.numpy as jnp
from jax import lax
from jax.experimental import pallas as pl
from jax.experimental.pallas import tpu as pltpu
from jax.sharding import PartitionSpec as P

CORES, CHIPS_Z, CHIPS_X = 2, 8, 4
ORDER_Z, ORDER_X = (7, 3, 6, 2, 5, 1, 4, 0), (3, 1, 2, 0)
ALONG_Z = [[z * CHIPS_X + x for z in ORDER_Z] for x in range(CHIPS_X)]
ALONG_X = [[z * CHIPS_X + x for x in ORDER_X] for z in range(CHIPS_Z)]
MIB = 1024 * 1024
LANES, MXU = 128, 256


def gather_by_exchange(value, groups):
    count = len(groups[0])
    copies = jnp.broadcast_to(value[None], (count, *value.shape))
    return lax.all_to_all(copies, "summa", 0, 0, axis_index_groups=groups, tiled=True)


def interleave(pairs, count):
    to = lax.broadcasted_iota(jnp.int32, (pairs * count, pairs * count), 0)
    of = lax.broadcasted_iota(jnp.int32, (pairs * count, pairs * count), 1)
    return (of == (to % pairs) * count + to // pairs).astype(jnp.float32).astype(jnp.bfloat16)


def rows_kernel(mask, window, row_tile, tiles, out, rows):
    x_count, windows, occ_rows, c_local, lanes = tiles.shape
    half, width = rows.shape[0], x_count * c_local
    summed = lanes // half
    blocks = lax.axis_size("perm") // CORES
    for i in range(occ_rows):
        for w in range(windows):
            tile = jnp.concatenate([tiles[ORDER_X.index(x), w, i] for x in range(x_count)], axis=0)
            tile = tile.astype(jnp.float32).T
            for k in range(summed):
                keep = mask[((i * summed + k) * blocks + row_tile[0]) * blocks + window[w]].astype(
                    jnp.float32
                )
                rows[:, i, pl.ds((k * windows + w) * width, width)] = (
                    tile[k * half : (k + 1) * half] * keep
                )
    out[...] = rows[...].reshape(out.shape).astype(out.dtype)


def amplitude_rows(tile_mask, window, row_tile, tiles):
    x_count, windows, occ_rows, c_local, lanes = tiles.shape
    summed = tile_mask.shape[1]
    half, depth = lanes // summed, summed * windows * x_count * c_local
    smem = pl.BlockSpec(memory_space=pltpu.SMEM)
    return pl.pallas_call(
        rows_kernel,
        out_shape=jax.ShapeDtypeStruct((half * occ_rows, depth), jnp.bfloat16),
        in_specs=[smem, smem, smem, pl.BlockSpec(memory_space=pltpu.VMEM)],
        out_specs=pl.BlockSpec(memory_space=pltpu.VMEM),
        scratch_shapes=[
            pltpu.VMEM((half, occ_rows, depth), jnp.float32),
        ],
        compiler_params=pltpu.CompilerParams(vmem_limit_bytes=16 * MIB),
    )(tile_mask.reshape(-1), window, row_tile, tiles)


def contract_kernel(
    panel_slot, window, lhs, row_energy, col_energy, slots, out, panels, done, came, left
):
    row_count, depth = lhs.shape
    halves, count, cols, width, lanes = panels.shape
    windows = window.shape[0]
    summed = count // windows
    blocks = panel_slot.shape[0] // summed
    fetches = [
        [
            pltpu.make_async_copy(
                slots.at[panel_slot[k * blocks + window[w]], :, :, pl.ds(n * lanes, lanes)],
                panels.at[n, k * windows + w],
                came.at[n, k * windows + w],
            )
            for k in range(summed)
            for w in range(windows)
        ]
        for n in range(halves)
    ]
    for fetch in fetches[0]:
        fetch.start()
    together = MXU // cols
    order = interleave(cols, together)
    stores = []
    for n in range(halves):
        for fetch in fetches[n]:
            fetch.wait()
        for fetch in sum(fetches[n + 1 : n + 2], []):
            fetch.start()
        for first in range(0, lanes, MXU):
            here = n * lanes + first
            rounded = []
            for j in range(cols):
                term = jnp.dot(
                    lhs[...],
                    panels[n, :, j, :, pl.ds(first, MXU)].reshape(depth, MXU),
                    preferred_element_type=jnp.float32,
                )
                parts = []
                for part in range(MXU // LANES):
                    gap = row_energy[...] + col_energy[pl.ds(j, 1), pl.ds(here + part * LANES, LANES)]
                    guess = pl.reciprocal(gap, approx=True)
                    parts.append(
                        term[:, part * LANES : (part + 1) * LANES] * (guess * (2.0 - gap * guess))
                    )
                rounded.append(jnp.concatenate(parts, axis=1).astype(out.dtype))
            for m in range(0, row_count, together):
                apart = jnp.concatenate([value[m : m + together] for value in rounded], axis=0)
                mixed = jnp.dot(order, apart, preferred_element_type=jnp.float32).astype(out.dtype)
                for part in range(MXU // LANES):
                    flat = done.at[here // LANES + part].reshape(row_count * cols, LANES)
                    flat[pl.ds(m * cols, MXU), :] = mixed[:, part * LANES : (part + 1) * LANES]
            for part in range(here // LANES, here // LANES + MXU // LANES):
                stores.append(
                    pltpu.make_async_copy(
                        done.at[part], out.at[:, :, pl.ds(part * LANES, LANES)], left.at[part]
                    )
                )
                stores[-1].start()
    for store in stores:
        store.wait()


def contract(panel_slot, window, lhs, row_energy, col_energy, slots):
    row_count, depth = lhs.shape
    _, cols, width, width_virt = slots.shape
    count, parts, halves = depth // width, width_virt // LANES, width_virt // MXU
    smem, vmem = pl.BlockSpec(memory_space=pltpu.SMEM), pl.BlockSpec(memory_space=pltpu.VMEM)
    hbm = pl.BlockSpec(memory_space=pltpu.HBM)
    return pl.pallas_call(
        contract_kernel,
        out_shape=jax.ShapeDtypeStruct((row_count, cols, width_virt), jnp.bfloat16),
        in_specs=[smem] * 2 + [vmem] * 3 + [hbm],
        out_specs=hbm,
        scratch_shapes=[
            pltpu.VMEM((halves, count, cols, width, width_virt // halves), slots.dtype),
            pltpu.VMEM((parts, row_count, cols, LANES), jnp.bfloat16),
            pltpu.SemaphoreType.DMA((halves, count)),
            pltpu.SemaphoreType.DMA((parts,)),
        ],
        compiler_params=pltpu.CompilerParams(vmem_limit_bytes=24 * MIB),
    )(
        panel_slot,
        window,
        lhs,
        row_energy,
        col_energy,
        pltpu.with_memory_space_constraint(slots, pltpu.HBM),
    )


def body(
    amplitudes,
    cycle_panels,
    tile_mask,
    panel_slot,
    window_blocks,
    virt_energy,
    row_energy,
    col_energy,
):
    _, _, col_local, width_virt = cycle_panels.shape
    c_local = amplitudes.shape[2]
    occ_rows, occ_summed = tile_mask.shape[:2]
    perm_count = lax.axis_size("perm")
    a_local = amplitudes.shape[1] // perm_count
    p = lax.axis_index("perm")

    slots = lax.all_gather(jnp.swapaxes(cycle_panels[0], 0, 1), "perm", axis=0)

    blocks = jnp.swapaxes(amplitudes[0].T.reshape(c_local, perm_count, a_local), 0, 1)
    blocks = lax.all_to_all(blocks, "perm", 0, 0, tiled=True)
    blocks, virt_energy, row_energy = lax.optimization_barrier((blocks, virt_energy, row_energy))
    blocks = blocks.reshape(occ_rows, occ_summed, c_local, a_local)
    blocks = jnp.concatenate([blocks[:, k] for k in range(occ_summed)], axis=-1)
    row_virt = lax.dynamic_slice_in_dim(virt_energy, p * a_local, a_local)
    rows = row_virt[:, None] - row_energy[None, :]
    rows = jnp.broadcast_to(rows[..., None], (*rows.shape, LANES)).reshape(-1, LANES)
    columns = virt_energy[None, :] - col_energy[:, None]
    tiles = gather_by_exchange(blocks, ALONG_Z)
    place = CHIPS_Z - 1 - window_blocks
    place = (place << 1 | place >> 2) & (CHIPS_Z - 1)
    tiles = jnp.stack(
        [lax.dynamic_index_in_dim(tiles, place[w], 0, False) for w in range(place.shape[0])]
    )
    tiles = gather_by_exchange(tiles, ALONG_X)
    tiles, rows, columns = lax.optimization_barrier((tiles, rows, columns))
    lhs = amplitude_rows(tile_mask, window_blocks, (p >> 1).reshape(1), tiles)
    result = contract(panel_slot, window_blocks, lhs, rows, columns, slots)
    return result.reshape(a_local, occ_rows, col_local, width_virt)


def solution(mesh):
    in_specs = (
        P("perm", None, "summa"),
        P("perm", None, "summa", None),
        P(),
        P(),
        P(),
        P(),
        P(),
        P("summa"),
    )
    out_specs = P("perm", None, "summa", None)
    return jax.shard_map(body, mesh=mesh, in_specs=in_specs, out_specs=out_specs, check_vma=False)
```

```python
import jax
import jax.numpy as jnp
from jax import lax
from jax.experimental import pallas as pl
from jax.experimental.pallas import tpu as pltpu
from jax.sharding import PartitionSpec as P

CORES, CHIPS_Z, CHIPS_X = 2, 8, 4
ORDER_Z, ORDER_X = (7, 3, 6, 2, 5, 1, 4, 0), (3, 1, 2, 0)
ALONG_Z = [[z * CHIPS_X + x for z in ORDER_Z] for x in range(CHIPS_X)]
ALONG_X = [[z * CHIPS_X + x for x in ORDER_X] for z in range(CHIPS_Z)]
MIB = 1024 * 1024
LANES, MXU = 128, 256


def gather_by_exchange(value, groups):
    count = len(groups[0])
    copies = jnp.broadcast_to(value[None], (count, *value.shape))
    return lax.all_to_all(copies, "summa", 0, 0, axis_index_groups=groups, tiled=True)


def interleave(pairs, count):
    to = lax.broadcasted_iota(jnp.int32, (pairs * count, pairs * count), 0)
    of = lax.broadcasted_iota(jnp.int32, (pairs * count, pairs * count), 1)
    return (of == (to % pairs) * count + to // pairs).astype(jnp.float32).astype(jnp.bfloat16)


def rows_kernel(mask, window, row_tile, tiles, out, rows):
    x_count, windows, occ_rows, c_local, lanes = tiles.shape
    half, width = rows.shape[0], x_count * c_local
    summed = lanes // half
    blocks = lax.axis_size("perm") // CORES
    for i in range(occ_rows):
        for w in range(windows):
            tile = jnp.concatenate([tiles[ORDER_X.index(x), w, i] for x in range(x_count)], axis=0)
            tile = tile.astype(jnp.float32).T
            for k in range(summed):
                keep = mask[((i * summed + k) * blocks + row_tile[0]) * blocks + window[w]].astype(
                    jnp.float32
                )
                rows[:, i, pl.ds((k * windows + w) * width, width)] = (
                    tile[k * half : (k + 1) * half] * keep
                )
    out[...] = rows[...].reshape(out.shape).astype(out.dtype)


def amplitude_rows(tile_mask, window, row_tile, tiles):
    x_count, windows, occ_rows, c_local, lanes = tiles.shape
    summed = tile_mask.shape[1]
    half, depth = lanes // summed, summed * windows * x_count * c_local
    smem = pl.BlockSpec(memory_space=pltpu.SMEM)
    return pl.pallas_call(
        rows_kernel,
        out_shape=jax.ShapeDtypeStruct((half * occ_rows, depth), jnp.bfloat16),
        in_specs=[smem, smem, smem, pl.BlockSpec(memory_space=pltpu.VMEM)],
        out_specs=pl.BlockSpec(memory_space=pltpu.VMEM),
        scratch_shapes=[
            pltpu.VMEM((half, occ_rows, depth), jnp.float32),
        ],
        compiler_params=pltpu.CompilerParams(vmem_limit_bytes=16 * MIB),
    )(tile_mask.reshape(-1), window, row_tile, tiles)


def contract_kernel(
    panel_slot, window, lhs, row_energy, col_energy, slots, out, panels, first, done, came, left
):
    row_count, depth = lhs.shape
    cols, count, width, width_virt = panels.shape
    windows = window.shape[0]
    summed = count // windows
    blocks = panel_slot.shape[0] // summed
    fetches = [
        pltpu.make_async_copy(
            slots.at[panel_slot[k * blocks + window[w]], j],
            panels.at[j, k * windows + w],
            came.at[j, k * windows + w],
        )
        for j in range(cols)
        for k in range(summed)
        for w in range(windows)
    ]
    for fetch in fetches:
        fetch.start()
    together = MXU // cols
    order = interleave(cols, together)
    steps = [(j, n) for j in range(cols) for n in range(0, width_virt, MXU)]
    stores = []

    def product(j, n):
        if n == 0:
            for fetch in fetches[j * count : (j + 1) * count]:
                fetch.wait()
        return jnp.dot(
            lhs[...],
            panels[j, :, :, pl.ds(n, MXU)].reshape(depth, MXU),
            preferred_element_type=jnp.float32,
        )

    def divided(term, j, n):
        parts = []
        for part in range(0, MXU, LANES):
            gap = row_energy[...] + col_energy[pl.ds(j, 1), pl.ds(n + part, LANES)]
            guess = pl.reciprocal(gap, approx=True)
            parts.append(term[:, part : part + LANES] * (guess * (2.0 - gap * guess)))
        return jnp.concatenate(parts, axis=1).astype(out.dtype)

    def finish(term, j, n):
        value = divided(term, j, n)
        if j < cols - 1:
            first[j, :, pl.ds(n, MXU)] = value
            return
        for m in range(0, row_count, together):
            apart = [first[before, pl.ds(m, together), pl.ds(n, MXU)] for before in range(cols - 1)]
            apart = jnp.concatenate(apart + [value[m : m + together]], axis=0)
            mixed = jnp.dot(order, apart, preferred_element_type=jnp.float32).astype(out.dtype)
            for part in range(MXU // LANES):
                flat = done.at[n // LANES + part].reshape(row_count * cols, LANES)
                flat[pl.ds(m * cols, MXU), :] = mixed[:, part * LANES : (part + 1) * LANES]
        for part in range(n // LANES, (n + MXU) // LANES):
            store = pltpu.make_async_copy(
                done.at[part], out.at[:, :, pl.ds(part * LANES, LANES)], left.at[part]
            )
            store.start()
            stores.append(store)

    term = product(*steps[0])
    for now, later in zip(steps, steps[1:] + [None]):
        ahead = product(*later) if later else None
        finish(term, *now)
        term = ahead
    for store in stores:
        store.wait()


def contract(panel_slot, window, lhs, row_energy, col_energy, slots):
    row_count, depth = lhs.shape
    _, cols, width, width_virt = slots.shape
    count, parts = depth // width, width_virt // LANES
    smem, vmem = pl.BlockSpec(memory_space=pltpu.SMEM), pl.BlockSpec(memory_space=pltpu.VMEM)
    hbm = pl.BlockSpec(memory_space=pltpu.HBM)
    return pl.pallas_call(
        contract_kernel,
        out_shape=jax.ShapeDtypeStruct((row_count, cols, width_virt), jnp.bfloat16),
        in_specs=[smem] * 2 + [vmem] * 3 + [hbm],
        out_specs=hbm,
        scratch_shapes=[
            pltpu.VMEM((cols, count, width, width_virt), slots.dtype),
            pltpu.VMEM((cols - 1, row_count, width_virt), jnp.bfloat16),
            pltpu.VMEM((parts, row_count, cols, LANES), jnp.bfloat16),
            pltpu.SemaphoreType.DMA((cols, count)),
            pltpu.SemaphoreType.DMA((parts,)),
        ],
        compiler_params=pltpu.CompilerParams(vmem_limit_bytes=24 * MIB),
    )(
        panel_slot,
        window,
        lhs,
        row_energy,
        col_energy,
        pltpu.with_memory_space_constraint(slots, pltpu.HBM),
    )


def body(
    amplitudes,
    cycle_panels,
    tile_mask,
    panel_slot,
    window_blocks,
    virt_energy,
    row_energy,
    col_energy,
):
    _, _, col_local, width_virt = cycle_panels.shape
    c_local = amplitudes.shape[2]
    occ_rows, occ_summed = tile_mask.shape[:2]
    perm_count = lax.axis_size("perm")
    a_local = amplitudes.shape[1] // perm_count
    p = lax.axis_index("perm")

    slots = lax.all_gather(jnp.swapaxes(cycle_panels[0], 0, 1), "perm", axis=0)

    blocks = jnp.swapaxes(amplitudes[0].T.reshape(c_local, perm_count, a_local), 0, 1)
    blocks = lax.all_to_all(blocks, "perm", 0, 0, tiled=True)
    blocks, virt_energy, row_energy = lax.optimization_barrier((blocks, virt_energy, row_energy))
    blocks = blocks.reshape(occ_rows, occ_summed, c_local, a_local)
    blocks = jnp.concatenate([blocks[:, k] for k in range(occ_summed)], axis=-1)
    row_virt = lax.dynamic_slice_in_dim(virt_energy, p * a_local, a_local)
    rows = row_virt[:, None] - row_energy[None, :]
    rows = jnp.broadcast_to(rows[..., None], (*rows.shape, LANES)).reshape(-1, LANES)
    columns = virt_energy[None, :] - col_energy[:, None]
    tiles = gather_by_exchange(blocks, ALONG_Z)
    place = CHIPS_Z - 1 - window_blocks
    place = (place << 1 | place >> 2) & (CHIPS_Z - 1)
    tiles = jnp.stack(
        [lax.dynamic_index_in_dim(tiles, place[w], 0, False) for w in range(place.shape[0])]
    )
    tiles = gather_by_exchange(tiles, ALONG_X)
    tiles, rows, columns = lax.optimization_barrier((tiles, rows, columns))
    lhs = amplitude_rows(tile_mask, window_blocks, (p >> 1).reshape(1), tiles)
    result = contract(panel_slot, window_blocks, lhs, rows, columns, slots)
    return result.reshape(a_local, occ_rows, col_local, width_virt)


def solution(mesh):
    in_specs = (
        P("perm", None, "summa"),
        P("perm", None, "summa", None),
        P(),
        P(),
        P(),
        P(),
        P(),
        P("summa"),
    )
    out_specs = P("perm", None, "summa", None)
    return jax.shard_map(body, mesh=mesh, in_specs=in_specs, out_specs=out_specs, check_vma=False)
```

```python
import jax
import jax.numpy as jnp
from jax import lax
from jax.experimental import pallas as pl
from jax.experimental.pallas import tpu as pltpu
from jax.sharding import PartitionSpec as P

CORES, CHIPS_Z, CHIPS_X = 2, 8, 4
ORDER_Z, ORDER_X = (7, 3, 6, 2, 5, 1, 4, 0), (3, 1, 2, 0)
ALONG_Z = [[z * CHIPS_X + x for z in ORDER_Z] for x in range(CHIPS_X)]
ALONG_X = [[z * CHIPS_X + x for x in ORDER_X] for z in range(CHIPS_Z)]
MIB = 1024 * 1024
LANES, MXU = 128, 256


def gather_by_exchange(value, groups):
    count = len(groups[0])
    copies = jnp.broadcast_to(value[None], (count, *value.shape))
    return lax.all_to_all(copies, "summa", 0, 0, axis_index_groups=groups, tiled=True)


def interleave(pairs, count):
    to = lax.broadcasted_iota(jnp.int32, (pairs * count, pairs * count), 0)
    of = lax.broadcasted_iota(jnp.int32, (pairs * count, pairs * count), 1)
    return (of == (to % pairs) * count + to // pairs).astype(jnp.float32).astype(jnp.bfloat16)


def rows_kernel(mask, window, row_tile, tiles, out, rows):
    x_count, windows, occ_rows, c_local, lanes = tiles.shape
    half, width = rows.shape[0], x_count * c_local
    summed = lanes // half
    blocks = lax.axis_size("perm") // CORES
    for i in range(occ_rows):
        for w in range(windows):
            tile = jnp.concatenate([tiles[ORDER_X.index(x), w, i] for x in range(x_count)], axis=0)
            tile = tile.astype(jnp.float32).T
            for k in range(summed):
                keep = mask[((i * summed + k) * blocks + row_tile[0]) * blocks + window[w]].astype(
                    jnp.float32
                )
                rows[:, i, pl.ds((k * windows + w) * width, width)] = (
                    tile[k * half : (k + 1) * half] * keep
                )
    out[...] = rows[...].reshape(out.shape).astype(out.dtype)


def amplitude_rows(tile_mask, window, row_tile, tiles):
    x_count, windows, occ_rows, c_local, lanes = tiles.shape
    summed = tile_mask.shape[1]
    half, depth = lanes // summed, summed * windows * x_count * c_local
    smem = pl.BlockSpec(memory_space=pltpu.SMEM)
    return pl.pallas_call(
        rows_kernel,
        out_shape=jax.ShapeDtypeStruct((half * occ_rows, depth), jnp.bfloat16),
        in_specs=[smem, smem, smem, pl.BlockSpec(memory_space=pltpu.VMEM)],
        out_specs=pl.BlockSpec(memory_space=pltpu.VMEM),
        scratch_shapes=[
            pltpu.VMEM((half, occ_rows, depth), jnp.float32),
        ],
        compiler_params=pltpu.CompilerParams(vmem_limit_bytes=16 * MIB),
    )(tile_mask.reshape(-1), window, row_tile, tiles)


def contract_kernel(
    panel_slot, window, lhs, row_energy, col_energy, slots, out, panels, first, done, came, left
):
    row_count, depth = lhs.shape
    cols, count, width, width_virt = panels.shape
    windows = window.shape[0]
    summed = count // windows
    blocks = panel_slot.shape[0] // summed
    fetches = [
        pltpu.make_async_copy(
            slots.at[panel_slot[k * blocks + window[w]], j],
            panels.at[j, k * windows + w],
            came.at[j, k * windows + w],
        )
        for j in range(cols)
        for k in range(summed)
        for w in range(windows)
    ]
    for fetch in fetches[:count]:
        fetch.start()
    together = MXU // cols
    order = interleave(cols, together)
    steps = [(j, n) for j in range(cols) for n in range(0, width_virt, MXU)]
    stores = []

    def product(j, n):
        if n == 0:
            for fetch in fetches[j * count : (j + 1) * count]:
                fetch.wait()
            for fetch in fetches[(j + 1) * count : (j + 2) * count]:
                fetch.start()
        return jnp.dot(
            lhs[...],
            panels[j, :, :, pl.ds(n, MXU)].reshape(depth, MXU),
            preferred_element_type=jnp.float32,
        )

    def divided(term, j, n):
        parts = []
        for part in range(0, MXU, LANES):
            gap = row_energy[...] + col_energy[pl.ds(j, 1), pl.ds(n + part, LANES)]
            guess = pl.reciprocal(gap, approx=True)
            parts.append(term[:, part : part + LANES] * (guess * (2.0 - gap * guess)))
        return jnp.concatenate(parts, axis=1).astype(out.dtype)

    def finish(term, j, n):
        value = divided(term, j, n)
        if j < cols - 1:
            first[j, :, pl.ds(n, MXU)] = value
            return
        for m in range(0, row_count, together):
            apart = [first[before, pl.ds(m, together), pl.ds(n, MXU)] for before in range(cols - 1)]
            apart = jnp.concatenate(apart + [value[m : m + together]], axis=0)
            mixed = jnp.dot(order, apart, preferred_element_type=jnp.float32).astype(out.dtype)
            for part in range(MXU // LANES):
                flat = done.at[n // LANES + part].reshape(row_count * cols, LANES)
                flat[pl.ds(m * cols, MXU), :] = mixed[:, part * LANES : (part + 1) * LANES]
        for part in range(n // LANES, (n + MXU) // LANES):
            store = pltpu.make_async_copy(
                done.at[part], out.at[:, :, pl.ds(part * LANES, LANES)], left.at[part]
            )
            store.start()
            stores.append(store)

    term = product(*steps[0])
    for now, later in zip(steps, steps[1:] + [None]):
        ahead = product(*later) if later else None
        finish(term, *now)
        term = ahead
    for store in stores:
        store.wait()


def contract(panel_slot, window, lhs, row_energy, col_energy, slots):
    row_count, depth = lhs.shape
    _, cols, width, width_virt = slots.shape
    count, parts = depth // width, width_virt // LANES
    smem, vmem = pl.BlockSpec(memory_space=pltpu.SMEM), pl.BlockSpec(memory_space=pltpu.VMEM)
    hbm = pl.BlockSpec(memory_space=pltpu.HBM)
    return pl.pallas_call(
        contract_kernel,
        out_shape=jax.ShapeDtypeStruct((row_count, cols, width_virt), jnp.bfloat16),
        in_specs=[smem] * 2 + [vmem] * 3 + [hbm],
        out_specs=hbm,
        scratch_shapes=[
            pltpu.VMEM((cols, count, width, width_virt), slots.dtype),
            pltpu.VMEM((cols - 1, row_count, width_virt), jnp.bfloat16),
            pltpu.VMEM((parts, row_count, cols, LANES), jnp.bfloat16),
            pltpu.SemaphoreType.DMA((cols, count)),
            pltpu.SemaphoreType.DMA((parts,)),
        ],
        compiler_params=pltpu.CompilerParams(vmem_limit_bytes=24 * MIB),
    )(
        panel_slot,
        window,
        lhs,
        row_energy,
        col_energy,
        pltpu.with_memory_space_constraint(slots, pltpu.HBM),
    )


def body(
    amplitudes,
    cycle_panels,
    tile_mask,
    panel_slot,
    window_blocks,
    virt_energy,
    row_energy,
    col_energy,
):
    _, _, col_local, width_virt = cycle_panels.shape
    c_local = amplitudes.shape[2]
    occ_rows, occ_summed = tile_mask.shape[:2]
    perm_count = lax.axis_size("perm")
    a_local = amplitudes.shape[1] // perm_count
    p = lax.axis_index("perm")

    slots = lax.all_gather(jnp.swapaxes(cycle_panels[0], 0, 1), "perm", axis=0)

    blocks = jnp.swapaxes(amplitudes[0].T.reshape(c_local, perm_count, a_local), 0, 1)
    blocks = lax.all_to_all(blocks, "perm", 0, 0, tiled=True)
    blocks, virt_energy, row_energy = lax.optimization_barrier((blocks, virt_energy, row_energy))
    blocks = blocks.reshape(occ_rows, occ_summed, c_local, a_local)
    blocks = jnp.concatenate([blocks[:, k] for k in range(occ_summed)], axis=-1)
    row_virt = lax.dynamic_slice_in_dim(virt_energy, p * a_local, a_local)
    rows = row_virt[:, None] - row_energy[None, :]
    rows = jnp.broadcast_to(rows[..., None], (*rows.shape, LANES)).reshape(-1, LANES)
    columns = virt_energy[None, :] - col_energy[:, None]
    tiles = gather_by_exchange(blocks, ALONG_Z)
    place = CHIPS_Z - 1 - window_blocks
    place = (place << 1 | place >> 2) & (CHIPS_Z - 1)
    tiles = jnp.stack(
        [lax.dynamic_index_in_dim(tiles, place[w], 0, False) for w in range(place.shape[0])]
    )
    tiles = gather_by_exchange(tiles, ALONG_X)
    tiles, rows, columns = lax.optimization_barrier((tiles, rows, columns))
    lhs = amplitude_rows(tile_mask, window_blocks, (p >> 1).reshape(1), tiles)
    result = contract(panel_slot, window_blocks, lhs, rows, columns, slots)
    return result.reshape(a_local, occ_rows, col_local, width_virt)


def solution(mesh):
    in_specs = (
        P("perm", None, "summa"),
        P("perm", None, "summa", None),
        P(),
        P(),
        P(),
        P(),
        P(),
        P("summa"),
    )
    out_specs = P("perm", None, "summa", None)
    return jax.shard_map(body, mesh=mesh, in_specs=in_specs, out_specs=out_specs, check_vma=False)
```

```python
import jax
import jax.numpy as jnp
from jax import lax
from jax.experimental import pallas as pl
from jax.experimental.pallas import tpu as pltpu
from jax.sharding import PartitionSpec as P

CORES, CHIPS_Z, CHIPS_X = 2, 8, 4
ORDER_Z, ORDER_X = (7, 3, 6, 2, 5, 1, 4, 0), (3, 1, 2, 0)
ALONG_Z = [[z * CHIPS_X + x for z in ORDER_Z] for x in range(CHIPS_X)]
ALONG_X = [[z * CHIPS_X + x for x in ORDER_X] for z in range(CHIPS_Z)]
MIB = 1024 * 1024
LANES, MXU = 128, 256


def gather_by_exchange(value, groups):
    count = len(groups[0])
    copies = jnp.broadcast_to(value[None], (count, *value.shape))
    return lax.all_to_all(copies, "summa", 0, 0, axis_index_groups=groups, tiled=True)


def together(parts, cols, some):
    count = parts * cols * some
    to = lax.broadcasted_iota(jnp.int32, (count, count), 0)
    of = lax.broadcasted_iota(jnp.int32, (count, count), 1)
    here = of == to % (parts * cols) * some + to // (parts * cols)
    return here.astype(jnp.float32).astype(jnp.bfloat16)


def rows_kernel(mask, window, row_tile, tiles, out, rows):
    x_count, windows, occ_rows, c_local, lanes = tiles.shape
    half, width = rows.shape[0], x_count * c_local
    summed = lanes // half
    blocks = lax.axis_size("perm") // CORES
    for i in range(occ_rows):
        for w in range(windows):
            tile = jnp.concatenate([tiles[ORDER_X.index(x), w, i] for x in range(x_count)], axis=0)
            tile = tile.astype(jnp.float32).T
            for k in range(summed):
                keep = mask[((i * summed + k) * blocks + row_tile[0]) * blocks + window[w]].astype(
                    jnp.float32
                )
                rows[:, i, pl.ds((k * windows + w) * width, width)] = (
                    tile[k * half : (k + 1) * half] * keep
                )
    out[...] = rows[...].reshape(out.shape).astype(out.dtype)


def amplitude_rows(tile_mask, window, row_tile, tiles):
    x_count, windows, occ_rows, c_local, lanes = tiles.shape
    summed = tile_mask.shape[1]
    half, depth = lanes // summed, summed * windows * x_count * c_local
    smem = pl.BlockSpec(memory_space=pltpu.SMEM)
    return pl.pallas_call(
        rows_kernel,
        out_shape=jax.ShapeDtypeStruct((half * occ_rows, depth), jnp.bfloat16),
        in_specs=[smem, smem, smem, pl.BlockSpec(memory_space=pltpu.VMEM)],
        out_specs=pl.BlockSpec(memory_space=pltpu.VMEM),
        scratch_shapes=[
            pltpu.VMEM((half, occ_rows, depth), jnp.float32),
        ],
        compiler_params=pltpu.CompilerParams(vmem_limit_bytes=16 * MIB),
    )(tile_mask.reshape(-1), window, row_tile, tiles)


def contract_kernel(
    panel_slot, window, lhs, row_energy, col_energy, slots, out, panels, values, done, came, left
):
    row_count, depth = lhs.shape
    cols, count, _, _ = panels.shape
    width = depth // count
    parts = panels.shape[2] // width
    windows = window.shape[0]
    summed = count // windows
    blocks = panel_slot.shape[0] // summed
    fetches = [
        pltpu.make_async_copy(
            slots.at[panel_slot[k * blocks + window[w]], pl.ds(j * parts * width, parts * width)],
            panels.at[j, k * windows + w],
            came.at[j, k * windows + w],
        )
        for j in range(cols)
        for k in range(summed)
        for w in range(windows)
    ]
    for fetch in fetches:
        fetch.start()
    beside = MXU // LANES
    some = MXU // (parts * cols)
    order = together(parts, cols, some)
    steps = [(j, part) for j in range(cols) for part in range(0, parts, beside)]

    def product(j, part):
        if part == 0:
            for fetch in fetches[j * count : (j + 1) * count]:
                fetch.wait()
        rhs = [
            panels[j, :, pl.ds(one * width, width), :].reshape(depth, LANES)
            for one in range(part, part + beside)
        ]
        return jnp.dot(
            lhs[...], jnp.concatenate(rhs, axis=1), preferred_element_type=jnp.float32
        )

    def finish(term, j, part):
        for one in range(beside):
            gap = row_energy[...] + col_energy[pl.ds(j, 1), pl.ds((part + one) * LANES, LANES)]
            guess = pl.reciprocal(gap, approx=True)
            value = term[:, one * LANES : (one + 1) * LANES] * (guess * (2.0 - gap * guess))
            values[part + one, j] = value.astype(out.dtype)

    term = product(*steps[0])
    for now, later in zip(steps, steps[1:] + [None]):
        ahead = product(*later) if later else None
        finish(term, *now)
        term = ahead
    stores = []
    rows_of = parts * cols
    span = row_count // left.shape[0]
    for m in range(0, row_count, some * beside):
        apart = [
            jnp.concatenate(
                [
                    values[part, j, pl.ds(m + one * some, some), :]
                    for part in range(parts)
                    for j in range(cols)
                ],
                axis=0,
            )
            for one in range(beside)
        ]
        mixed = jnp.dot(order, jnp.concatenate(apart, axis=1), preferred_element_type=jnp.float32)
        mixed = mixed.astype(out.dtype)
        for one in range(beside):
            done[pl.ds((m + one * some) * rows_of, MXU), :] = mixed[:, one * LANES : (one + 1) * LANES]
        if (m + some * beside) % span == 0:
            rows = pl.ds((m + some * beside - span) * rows_of, span * rows_of)
            store = pltpu.make_async_copy(done.at[rows], out.at[rows], left.at[m // span])
            store.start()
            stores.append(store)
    for store in stores:
        store.wait()


def contract(panel_slot, window, lhs, row_energy, col_energy, slots):
    row_count, depth = lhs.shape
    cols, width_virt = col_energy.shape
    parts = width_virt // LANES
    width = slots.shape[1] // (parts * cols)
    count = depth // width
    smem, vmem = pl.BlockSpec(memory_space=pltpu.SMEM), pl.BlockSpec(memory_space=pltpu.VMEM)
    hbm = pl.BlockSpec(memory_space=pltpu.HBM)
    return pl.pallas_call(
        contract_kernel,
        out_shape=jax.ShapeDtypeStruct((row_count * parts * cols, LANES), jnp.bfloat16),
        in_specs=[smem] * 2 + [vmem] * 3 + [hbm],
        out_specs=hbm,
        scratch_shapes=[
            pltpu.VMEM((cols, count, parts * width, LANES), slots.dtype),
            pltpu.VMEM((parts, cols, row_count, LANES), jnp.bfloat16),
            pltpu.VMEM((row_count * parts * cols, LANES), jnp.bfloat16),
            pltpu.SemaphoreType.DMA((cols, count)),
            pltpu.SemaphoreType.DMA((8,)),
        ],
        compiler_params=pltpu.CompilerParams(vmem_limit_bytes=24 * MIB),
    )(
        panel_slot,
        window,
        lhs,
        row_energy,
        col_energy,
        pltpu.with_memory_space_constraint(slots, pltpu.HBM),
    )


def body(
    amplitudes,
    cycle_panels,
    tile_mask,
    panel_slot,
    window_blocks,
    virt_energy,
    row_energy,
    col_energy,
):
    _, _, col_local, width_virt = cycle_panels.shape
    c_local = amplitudes.shape[2]
    occ_rows, occ_summed = tile_mask.shape[:2]
    perm_count = lax.axis_size("perm")
    a_local = amplitudes.shape[1] // perm_count
    p = lax.axis_index("perm")

    width, parts = cycle_panels.shape[1], width_virt // LANES
    as_given = jnp.swapaxes(cycle_panels.reshape(width, col_local, parts, LANES), 1, 2)
    as_given = lax.optimization_barrier(as_given.reshape(-1, LANES))
    by_part = jnp.transpose(as_given.reshape(width, parts, col_local, LANES), (2, 1, 0, 3))
    slots = lax.all_gather(by_part.reshape(-1, LANES), "perm", axis=0)

    blocks = jnp.swapaxes(amplitudes[0].T.reshape(c_local, perm_count, a_local), 0, 1)
    blocks = lax.all_to_all(blocks, "perm", 0, 0, tiled=True)
    blocks, virt_energy, row_energy = lax.optimization_barrier((blocks, virt_energy, row_energy))
    blocks = blocks.reshape(occ_rows, occ_summed, c_local, a_local)
    blocks = jnp.concatenate([blocks[:, k] for k in range(occ_summed)], axis=-1)
    row_virt = lax.dynamic_slice_in_dim(virt_energy, p * a_local, a_local)
    rows = row_virt[:, None] - row_energy[None, :]
    rows = jnp.broadcast_to(rows[..., None], (*rows.shape, LANES)).reshape(-1, LANES)
    columns = virt_energy[None, :] - col_energy[:, None]
    tiles = gather_by_exchange(blocks, ALONG_Z)
    place = CHIPS_Z - 1 - window_blocks
    place = (place << 1 | place >> 2) & (CHIPS_Z - 1)
    tiles = jnp.stack(
        [lax.dynamic_index_in_dim(tiles, place[w], 0, False) for w in range(place.shape[0])]
    )
    tiles = gather_by_exchange(tiles, ALONG_X)
    tiles, rows, columns = lax.optimization_barrier((tiles, rows, columns))
    lhs = amplitude_rows(tile_mask, window_blocks, (p >> 1).reshape(1), tiles)
    result = contract(panel_slot, window_blocks, lhs, rows, columns, slots)
    result = jnp.swapaxes(result.reshape(-1, parts, col_local, LANES), 1, 2)
    return result.reshape(a_local, occ_rows, col_local, width_virt)


def solution(mesh):
    in_specs = (
        P("perm", None, "summa"),
        P("perm", None, "summa", None),
        P(),
        P(),
        P(),
        P(),
        P(),
        P("summa"),
    )
    out_specs = P("perm", None, "summa", None)
    return jax.shard_map(body, mesh=mesh, in_specs=in_specs, out_specs=out_specs, check_vma=False)
```

```python
import jax
import jax.numpy as jnp
from jax import lax
from jax.experimental import pallas as pl
from jax.experimental.pallas import tpu as pltpu
from jax.sharding import PartitionSpec as P

CORES, CHIPS_Z, CHIPS_X = 2, 8, 4
ORDER_Z, ORDER_X = (7, 3, 6, 2, 4, 0, 5, 1), (3, 1, 2, 0)
ALONG_Z = [[z * CHIPS_X + x for z in ORDER_Z] for x in range(CHIPS_X)]
ALONG_X = [[z * CHIPS_X + x for x in ORDER_X] for z in range(CHIPS_Z)]
MIB = 1024 * 1024
LANES, MXU = 128, 256


def gather_by_exchange(value, groups):
    count = len(groups[0])
    copies = jnp.broadcast_to(value[None], (count, *value.shape))
    return lax.all_to_all(copies, "summa", 0, 0, axis_index_groups=groups, tiled=True)


def together(parts, cols, some):
    count = parts * cols * some
    to = lax.broadcasted_iota(jnp.int32, (count, count), 0)
    of = lax.broadcasted_iota(jnp.int32, (count, count), 1)
    here = of == to % (parts * cols) * some + to // (parts * cols)
    return here.astype(jnp.float32).astype(jnp.bfloat16)


def rows_kernel(mask, window, row_tile, tiles, out, rows):
    x_count, windows, occ_rows, c_local, lanes = tiles.shape
    half, width = rows.shape[0], x_count * c_local
    summed = lanes // half
    blocks = lax.axis_size("perm") // CORES
    for i in range(occ_rows):
        for w in range(windows):
            tile = jnp.concatenate([tiles[ORDER_X.index(x), w, i] for x in range(x_count)], axis=0)
            tile = tile.astype(jnp.float32).T
            for k in range(summed):
                keep = mask[((i * summed + k) * blocks + row_tile[0]) * blocks + window[w]].astype(
                    jnp.float32
                )
                rows[:, i, pl.ds((k * windows + w) * width, width)] = (
                    tile[k * half : (k + 1) * half] * keep
                )
    out[...] = rows[...].reshape(out.shape).astype(out.dtype)


def amplitude_rows(tile_mask, window, row_tile, tiles):
    x_count, windows, occ_rows, c_local, lanes = tiles.shape
    summed = tile_mask.shape[1]
    half, depth = lanes // summed, summed * windows * x_count * c_local
    smem = pl.BlockSpec(memory_space=pltpu.SMEM)
    return pl.pallas_call(
        rows_kernel,
        out_shape=jax.ShapeDtypeStruct((half * occ_rows, depth), jnp.bfloat16),
        in_specs=[smem, smem, smem, pl.BlockSpec(memory_space=pltpu.VMEM)],
        out_specs=pl.BlockSpec(memory_space=pltpu.VMEM),
        scratch_shapes=[
            pltpu.VMEM((half, occ_rows, depth), jnp.float32),
        ],
        compiler_params=pltpu.CompilerParams(vmem_limit_bytes=16 * MIB),
    )(tile_mask.reshape(-1), window, row_tile, tiles)


def contract_kernel(
    panel_slot, window, lhs, row_energy, col_energy, slots, out, panels, values, done, came, left
):
    row_count, depth = lhs.shape
    cols, count, _, _ = panels.shape
    width = depth // count
    parts = panels.shape[2] // width
    windows = window.shape[0]
    summed = count // windows
    blocks = panel_slot.shape[0] // summed
    beside = MXU // LANES
    pieces = [(0, 0, beside), (0, beside, parts)] + [(j, 0, parts) for j in range(1, cols)]
    fetches = [
        [
            pltpu.make_async_copy(
                slots.at[
                    panel_slot[k * blocks + window[w]],
                    pl.ds((j * parts + low) * width, (high - low) * width),
                ],
                panels.at[j, k * windows + w, pl.ds(low * width, (high - low) * width)],
                came.at[n, k * windows + w],
            )
            for k in range(summed)
            for w in range(windows)
        ]
        for n, (j, low, high) in enumerate(pieces)
    ]
    for fetch in sum(fetches, []):
        fetch.start()
    some = MXU // (parts * cols)
    order = together(parts, cols, some)
    steps = [(j, part) for j in range(cols) for part in range(0, parts, beside)]

    def product(j, part):
        for fetch, (of, low, _) in zip(fetches, pieces):
            if (of, low) == (j, part):
                for one in fetch:
                    one.wait()
        rhs = [
            panels[j, :, pl.ds(one * width, width), :].reshape(depth, LANES)
            for one in range(part, part + beside)
        ]
        return jnp.dot(
            lhs[...], jnp.concatenate(rhs, axis=1), preferred_element_type=jnp.float32
        )

    def finish(term, j, part):
        for one in range(beside):
            gap = row_energy[...] + col_energy[pl.ds(j, 1), pl.ds((part + one) * LANES, LANES)]
            guess = pl.reciprocal(gap, approx=True)
            value = term[:, one * LANES : (one + 1) * LANES] * (guess * (2.0 - gap * guess))
            values[part + one, j] = value.astype(out.dtype)

    term = product(*steps[0])
    for now, later in zip(steps, steps[1:] + [None]):
        ahead = product(*later) if later else None
        finish(term, *now)
        term = ahead
    stores = []
    rows_of = parts * cols
    span = row_count // left.shape[0]
    for m in range(0, row_count, some * beside):
        apart = [
            jnp.concatenate(
                [
                    values[part, j, pl.ds(m + one * some, some), :]
                    for part in range(parts)
                    for j in range(cols)
                ],
                axis=0,
            )
            for one in range(beside)
        ]
        mixed = jnp.dot(order, jnp.concatenate(apart, axis=1), preferred_element_type=jnp.float32)
        mixed = mixed.astype(out.dtype)
        for one in range(beside):
            done[pl.ds((m + one * some) * rows_of, MXU), :] = mixed[:, one * LANES : (one + 1) * LANES]
        if (m + some * beside) % span == 0:
            rows = pl.ds((m + some * beside - span) * rows_of, span * rows_of)
            store = pltpu.make_async_copy(done.at[rows], out.at[rows], left.at[m // span])
            store.start()
            stores.append(store)
    for store in stores:
        store.wait()


def contract(panel_slot, window, lhs, row_energy, col_energy, slots):
    row_count, depth = lhs.shape
    cols, width_virt = col_energy.shape
    parts = width_virt // LANES
    width = slots.shape[1] // (parts * cols)
    count = depth // width
    smem, vmem = pl.BlockSpec(memory_space=pltpu.SMEM), pl.BlockSpec(memory_space=pltpu.VMEM)
    hbm = pl.BlockSpec(memory_space=pltpu.HBM)
    return pl.pallas_call(
        contract_kernel,
        out_shape=jax.ShapeDtypeStruct((row_count * parts * cols, LANES), jnp.bfloat16),
        in_specs=[smem] * 2 + [vmem] * 3 + [hbm],
        out_specs=hbm,
        scratch_shapes=[
            pltpu.VMEM((cols, count, parts * width, LANES), slots.dtype),
            pltpu.VMEM((parts, cols, row_count, LANES), jnp.bfloat16),
            pltpu.VMEM((row_count * parts * cols, LANES), jnp.bfloat16),
            pltpu.SemaphoreType.DMA((cols + 1, count)),
            pltpu.SemaphoreType.DMA((8,)),
        ],
        compiler_params=pltpu.CompilerParams(vmem_limit_bytes=24 * MIB),
    )(
        panel_slot,
        window,
        lhs,
        row_energy,
        col_energy,
        pltpu.with_memory_space_constraint(slots, pltpu.HBM),
    )


def body(
    amplitudes,
    cycle_panels,
    tile_mask,
    panel_slot,
    window_blocks,
    virt_energy,
    row_energy,
    col_energy,
):
    _, _, col_local, width_virt = cycle_panels.shape
    c_local = amplitudes.shape[2]
    occ_rows, occ_summed = tile_mask.shape[:2]
    perm_count = lax.axis_size("perm")
    a_local = amplitudes.shape[1] // perm_count
    p = lax.axis_index("perm")

    width, parts = cycle_panels.shape[1], width_virt // LANES
    as_given = jnp.swapaxes(cycle_panels.reshape(width, col_local, parts, LANES), 1, 2)
    as_given = lax.optimization_barrier(as_given.reshape(-1, LANES))
    by_part = jnp.transpose(as_given.reshape(width, parts, col_local, LANES), (2, 1, 0, 3))
    slots = lax.all_gather(by_part.reshape(-1, LANES), "perm", axis=0)

    blocks = jnp.swapaxes(amplitudes[0].T.reshape(c_local, perm_count, a_local), 0, 1)
    blocks = lax.all_to_all(blocks, "perm", 0, 0, tiled=True)
    blocks, virt_energy, row_energy = lax.optimization_barrier((blocks, virt_energy, row_energy))
    blocks = blocks.reshape(occ_rows, occ_summed, c_local, a_local)
    blocks = jnp.concatenate([blocks[:, k] for k in range(occ_summed)], axis=-1)
    row_virt = lax.dynamic_slice_in_dim(virt_energy, p * a_local, a_local)
    rows = row_virt[:, None] - row_energy[None, :]
    rows = jnp.broadcast_to(rows[..., None], (*rows.shape, LANES)).reshape(-1, LANES)
    columns = virt_energy[None, :] - col_energy[:, None]
    tiles = gather_by_exchange(blocks, ALONG_Z)
    place = jnp.array([ORDER_Z.index(z) for z in range(CHIPS_Z)], jnp.int32)[window_blocks]
    tiles = jnp.stack(
        [lax.dynamic_index_in_dim(tiles, place[w], 0, False) for w in range(place.shape[0])]
    )
    tiles = gather_by_exchange(tiles, ALONG_X)
    tiles, rows, columns = lax.optimization_barrier((tiles, rows, columns))
    lhs = amplitude_rows(tile_mask, window_blocks, (p >> 1).reshape(1), tiles)
    result = contract(panel_slot, window_blocks, lhs, rows, columns, slots)
    result = jnp.swapaxes(result.reshape(-1, parts, col_local, LANES), 1, 2)
    return result.reshape(a_local, occ_rows, col_local, width_virt)


def solution(mesh):
    in_specs = (
        P("perm", None, "summa"),
        P("perm", None, "summa", None),
        P(),
        P(),
        P(),
        P(),
        P(),
        P("summa"),
    )
    out_specs = P("perm", None, "summa", None)
    return jax.shard_map(body, mesh=mesh, in_specs=in_specs, out_specs=out_specs, check_vma=False)
```

```python
import jax
import jax.numpy as jnp
from jax import lax
from jax.experimental import pallas as pl
from jax.experimental.pallas import tpu as pltpu
from jax.sharding import PartitionSpec as P

CORES, CHIPS_Z, CHIPS_X = 2, 8, 4
ORDER_Z, ORDER_X = (7, 3, 6, 2, 5, 1, 4, 0), (3, 1, 2, 0)
ALONG_Z = [[z * CHIPS_X + x for z in ORDER_Z] for x in range(CHIPS_X)]
ALONG_X = [[z * CHIPS_X + x for x in ORDER_X] for z in range(CHIPS_Z)]
MIB = 1024 * 1024
LANES, MXU = 128, 256


def gather_by_exchange(value, groups):
    count = len(groups[0])
    copies = jnp.broadcast_to(value[None], (count, *value.shape))
    return lax.all_to_all(copies, "summa", 0, 0, axis_index_groups=groups, tiled=True)


def together(parts, cols, some):
    count = parts * cols * some
    to = lax.broadcasted_iota(jnp.int32, (count, count), 0)
    of = lax.broadcasted_iota(jnp.int32, (count, count), 1)
    here = of == to % (parts * cols) * some + to // (parts * cols)
    return here.astype(jnp.float32).astype(jnp.bfloat16)


def rows_kernel(keep, tiles, out, rows):
    x_count, windows, occ_rows, c_local, lanes = tiles.shape
    half, width = rows.shape[0], x_count * c_local
    summed = lanes // half
    for i in range(occ_rows):
        for w in range(windows):
            tile = jnp.concatenate([tiles[ORDER_X.index(x), w, i] for x in range(x_count)], axis=0)
            tile = tile.astype(jnp.float32).T
            for k in range(summed):
                rows[:, i, pl.ds((k * windows + w) * width, width)] = (
                    tile[k * half : (k + 1) * half] * keep[k * windows + w, pl.ds(i, 1), :]
                )
    out[...] = rows[...].reshape(out.shape).astype(out.dtype)


def amplitude_rows(keep, tiles):
    x_count, windows, occ_rows, c_local, lanes = tiles.shape
    summed = keep.shape[0] // windows
    half, depth = lanes // summed, summed * windows * x_count * c_local
    vmem = pl.BlockSpec(memory_space=pltpu.VMEM)
    return pl.pallas_call(
        rows_kernel,
        out_shape=jax.ShapeDtypeStruct((half * occ_rows, depth), jnp.bfloat16),
        in_specs=[vmem, vmem],
        out_specs=vmem,
        scratch_shapes=[pltpu.VMEM((half, occ_rows, depth), jnp.float32)],
        compiler_params=pltpu.CompilerParams(vmem_limit_bytes=16 * MIB),
    )(keep, tiles)


def contract_kernel(
    chosen, lhs, row_energy, col_energy, slots, out, panels, values, done, came, left
):
    row_count, depth = lhs.shape
    cols, count, _, _ = panels.shape
    width = depth // count
    parts = panels.shape[2] // width
    fetches = []
    slot = [jnp.max(chosen[pl.ds(m, 1), :]) for m in range(count)]
    for j in range(cols):
        for m in range(count):
            rows = pl.ds(j * parts * width, parts * width)
            fetches.append(
                pltpu.make_async_copy(slots.at[slot[m], rows], panels.at[j, m], came.at[j, m])
            )
    for fetch in fetches:
        fetch.start()
    beside = MXU // LANES
    some = MXU // (parts * cols)
    order = together(parts, cols, some)
    steps = [(j, part) for j in range(cols) for part in range(0, parts, beside)]

    def product(j, part):
        if part == 0:
            for fetch in fetches[j * count : (j + 1) * count]:
                fetch.wait()
        rhs = [
            panels[j, :, pl.ds(one * width, width), :].reshape(depth, LANES)
            for one in range(part, part + beside)
        ]
        return jnp.dot(
            lhs[...], jnp.concatenate(rhs, axis=1), preferred_element_type=jnp.float32
        )

    def finish(term, j, part):
        for one in range(beside):
            gap = row_energy[...] + col_energy[pl.ds(j, 1), pl.ds((part + one) * LANES, LANES)]
            guess = pl.reciprocal(gap, approx=True)
            value = term[:, one * LANES : (one + 1) * LANES] * (guess * (2.0 - gap * guess))
            values[part + one, j] = value.astype(out.dtype)

    term = product(*steps[0])
    for now, later in zip(steps, steps[1:] + [None]):
        ahead = product(*later) if later else None
        finish(term, *now)
        term = ahead
    stores = []
    rows_of = parts * cols
    span = row_count // left.shape[0]
    for m in range(0, row_count, some * beside):
        apart = [
            jnp.concatenate(
                [
                    values[part, j, pl.ds(m + one * some, some), :]
                    for part in range(parts)
                    for j in range(cols)
                ],
                axis=0,
            )
            for one in range(beside)
        ]
        mixed = jnp.dot(order, jnp.concatenate(apart, axis=1), preferred_element_type=jnp.float32)
        mixed = mixed.astype(out.dtype)
        for one in range(beside):
            done[pl.ds((m + one * some) * rows_of, MXU), :] = mixed[:, one * LANES : (one + 1) * LANES]
        if (m + some * beside) % span == 0:
            rows = pl.ds((m + some * beside - span) * rows_of, span * rows_of)
            store = pltpu.make_async_copy(done.at[rows], out.at[rows], left.at[m // span])
            store.start()
            stores.append(store)
    for store in stores:
        store.wait()


def contract(chosen, lhs, row_energy, col_energy, slots):
    row_count, depth = lhs.shape
    cols, width_virt = col_energy.shape
    parts = width_virt // LANES
    width = slots.shape[1] // (parts * cols)
    count = depth // width
    vmem = pl.BlockSpec(memory_space=pltpu.VMEM)
    hbm = pl.BlockSpec(memory_space=pltpu.HBM)
    return pl.pallas_call(
        contract_kernel,
        out_shape=jax.ShapeDtypeStruct((row_count * parts * cols, LANES), jnp.bfloat16),
        in_specs=[vmem] * 4 + [hbm],
        out_specs=hbm,
        scratch_shapes=[
            pltpu.VMEM((cols, count, parts * width, LANES), slots.dtype),
            pltpu.VMEM((parts, cols, row_count, LANES), jnp.bfloat16),
            pltpu.VMEM((row_count * parts * cols, LANES), jnp.bfloat16),
            pltpu.SemaphoreType.DMA((cols, count)),
            pltpu.SemaphoreType.DMA((8,)),
        ],
        compiler_params=pltpu.CompilerParams(vmem_limit_bytes=24 * MIB),
    )(
        chosen,
        lhs,
        row_energy,
        col_energy,
        pltpu.with_memory_space_constraint(slots, pltpu.HBM),
    )


def body(
    amplitudes,
    cycle_panels,
    tile_mask,
    panel_slot,
    window_blocks,
    virt_energy,
    row_energy,
    col_energy,
):
    _, _, col_local, width_virt = cycle_panels.shape
    c_local = amplitudes.shape[2]
    occ_rows, occ_summed = tile_mask.shape[:2]
    perm_count = lax.axis_size("perm")
    a_local = amplitudes.shape[1] // perm_count
    p = lax.axis_index("perm")

    width, parts = cycle_panels.shape[1], width_virt // LANES
    as_given = jnp.swapaxes(cycle_panels.reshape(width, col_local, parts, LANES), 1, 2)
    as_given = lax.optimization_barrier(as_given.reshape(-1, LANES))
    by_part = jnp.transpose(as_given.reshape(width, parts, col_local, LANES), (2, 1, 0, 3))
    slots = lax.all_gather(by_part.reshape(-1, LANES), "perm", axis=0)

    blocks = jnp.swapaxes(amplitudes[0].T.reshape(c_local, perm_count, a_local), 0, 1)
    blocks = lax.all_to_all(blocks, "perm", 0, 0, tiled=True)
    blocks, virt_energy, row_energy = lax.optimization_barrier((blocks, virt_energy, row_energy))
    blocks = blocks.reshape(occ_rows, occ_summed, c_local, a_local)
    blocks = jnp.concatenate([blocks[:, k] for k in range(occ_summed)], axis=-1)
    row_virt = lax.dynamic_slice_in_dim(virt_energy, p * a_local, a_local)
    rows = row_virt[:, None] - row_energy[None, :]
    rows = jnp.broadcast_to(rows[..., None], (*rows.shape, LANES)).reshape(-1, LANES)
    columns = virt_energy[None, :] - col_energy[:, None]
    tiles = gather_by_exchange(blocks, ALONG_Z)
    place = CHIPS_Z - 1 - window_blocks
    place = (place << 1 | place >> 2) & (CHIPS_Z - 1)
    tiles = jnp.stack(
        [lax.dynamic_index_in_dim(tiles, place[w], 0, False) for w in range(place.shape[0])]
    )
    tiles, tile_mask, panel_slot, window_blocks = lax.optimization_barrier(
        (tiles, tile_mask, panel_slot, window_blocks)
    )
    tiles = gather_by_exchange(tiles, ALONG_X)
    keep = lax.dynamic_index_in_dim(tile_mask, p // CORES, axis=2, keepdims=False)
    keep = jnp.take(keep, window_blocks, axis=2).transpose(1, 2, 0).reshape(-1, occ_rows)
    keep = jnp.broadcast_to(keep[..., None].astype(jnp.float32), (*keep.shape, LANES))
    chosen = jnp.take(panel_slot.reshape(occ_summed, -1), window_blocks, axis=1).reshape(-1)
    chosen = jnp.broadcast_to(chosen[:, None], (chosen.shape[0], LANES))
    tiles, rows, columns, keep, chosen = lax.optimization_barrier(
        (tiles, rows, columns, keep, chosen)
    )
    lhs = amplitude_rows(keep, tiles)
    result = contract(chosen, lhs, rows, columns, slots)
    result = jnp.swapaxes(result.reshape(-1, parts, col_local, LANES), 1, 2)
    return result.reshape(a_local, occ_rows, col_local, width_virt)


def solution(mesh):
    in_specs = (
        P("perm", None, "summa"),
        P("perm", None, "summa", None),
        P(),
        P(),
        P(),
        P(),
        P(),
        P("summa"),
    )
    out_specs = P("perm", None, "summa", None)
    return jax.shard_map(body, mesh=mesh, in_specs=in_specs, out_specs=out_specs, check_vma=False)
```

```python
import jax
import jax.numpy as jnp
from jax import lax
from jax.experimental import pallas as pl
from jax.experimental.pallas import tpu as pltpu
from jax.sharding import PartitionSpec as P

CORES, CHIPS_Z, CHIPS_X = 2, 8, 4
ORDER_Z, ORDER_X = (7, 3, 6, 2, 5, 1, 4, 0), (3, 1, 2, 0)
ALONG_Z = [[z * CHIPS_X + x for z in ORDER_Z] for x in range(CHIPS_X)]
ALONG_X = [[z * CHIPS_X + x for x in ORDER_X] for z in range(CHIPS_Z)]
MIB = 1024 * 1024
LANES, MXU = 128, 256


def gather_by_exchange(value, groups):
    count = len(groups[0])
    copies = jnp.broadcast_to(value[None], (count, *value.shape))
    return lax.all_to_all(copies, "summa", 0, 0, axis_index_groups=groups, tiled=True)


def together(parts, cols, some):
    count = parts * cols * some
    to = lax.broadcasted_iota(jnp.int32, (count, count), 0)
    of = lax.broadcasted_iota(jnp.int32, (count, count), 1)
    here = of == to % (parts * cols) * some + to // (parts * cols)
    return here.astype(jnp.float32).astype(jnp.bfloat16)


def rows_kernel(keep, tiles, out, rows):
    x_count, windows, occ_rows, c_local, lanes = tiles.shape
    half, width = rows.shape[0], x_count * c_local
    summed = lanes // half
    for i in range(occ_rows):
        for w in range(windows):
            tile = jnp.concatenate([tiles[ORDER_X.index(x), w, i] for x in range(x_count)], axis=0)
            tile = tile.astype(jnp.float32).T
            for k in range(summed):
                rows[:, i, pl.ds((k * windows + w) * width, width)] = (
                    tile[k * half : (k + 1) * half] * keep[k * windows + w, pl.ds(i, 1), :]
                )
    out[...] = rows[...].reshape(out.shape).astype(out.dtype)


def amplitude_rows(keep, tiles):
    x_count, windows, occ_rows, c_local, lanes = tiles.shape
    summed = keep.shape[0] // windows
    half, depth = lanes // summed, summed * windows * x_count * c_local
    vmem = pl.BlockSpec(memory_space=pltpu.VMEM)
    return pl.pallas_call(
        rows_kernel,
        out_shape=jax.ShapeDtypeStruct((half * occ_rows, depth), jnp.bfloat16),
        in_specs=[vmem, vmem],
        out_specs=vmem,
        scratch_shapes=[pltpu.VMEM((half, occ_rows, depth), jnp.float32)],
        compiler_params=pltpu.CompilerParams(vmem_limit_bytes=16 * MIB),
    )(keep, tiles)


def contract_kernel(
    chosen, lhs, row_energy, col_energy, slots, out, panels, values, done, came, left
):
    row_count, depth = lhs.shape
    cols, count, _, _ = panels.shape
    width = depth // count
    parts = panels.shape[2] // width
    fetches = []
    slot = [jnp.max(chosen[pl.ds(m, 1), :]) for m in range(count)]
    for j in range(cols):
        for m in range(count):
            rows = pl.ds(j * parts * width, parts * width)
            fetches.append(
                pltpu.make_async_copy(slots.at[slot[m], rows], panels.at[j, m], came.at[j, m])
            )
    for fetch in fetches:
        fetch.start()
    beside = MXU // LANES
    some = MXU // (parts * cols)
    order = together(parts, cols, some)
    wide = parts // 2
    steps = [(j, part) for j in range(cols) for part in range(0, parts, wide)]

    def product(j, part):
        if part == 0:
            for fetch in fetches[j * count : (j + 1) * count]:
                fetch.wait()
        rhs = [
            panels[j, :, pl.ds(one * width, width), :].reshape(depth, LANES)
            for one in range(part, part + wide)
        ]
        return jnp.dot(
            lhs[...], jnp.concatenate(rhs, axis=1), preferred_element_type=jnp.float32
        )

    def finish(term, j, part):
        for one in range(wide):
            gap = row_energy[...] + col_energy[pl.ds(j, 1), pl.ds((part + one) * LANES, LANES)]
            guess = pl.reciprocal(gap, approx=True)
            value = term[:, one * LANES : (one + 1) * LANES] * (guess * (2.0 - gap * guess))
            values[part + one, j] = value.astype(out.dtype)

    term = product(*steps[0])
    for now, later in zip(steps, steps[1:] + [None]):
        ahead = product(*later) if later else None
        finish(term, *now)
        term = ahead
    stores = []
    rows_of = parts * cols
    span = row_count // left.shape[0]
    for m in range(0, row_count, some * beside):
        apart = [
            jnp.concatenate(
                [
                    values[part, j, pl.ds(m + one * some, some), :]
                    for part in range(parts)
                    for j in range(cols)
                ],
                axis=0,
            )
            for one in range(beside)
        ]
        mixed = jnp.dot(order, jnp.concatenate(apart, axis=1), preferred_element_type=jnp.float32)
        mixed = mixed.astype(out.dtype)
        for one in range(beside):
            done[pl.ds((m + one * some) * rows_of, MXU), :] = mixed[:, one * LANES : (one + 1) * LANES]
        if (m + some * beside) % span == 0:
            rows = pl.ds((m + some * beside - span) * rows_of, span * rows_of)
            store = pltpu.make_async_copy(done.at[rows], out.at[rows], left.at[m // span])
            store.start()
            stores.append(store)
    for store in stores:
        store.wait()


def contract(chosen, lhs, row_energy, col_energy, slots):
    row_count, depth = lhs.shape
    cols, width_virt = col_energy.shape
    parts = width_virt // LANES
    width = slots.shape[1] // (parts * cols)
    count = depth // width
    vmem = pl.BlockSpec(memory_space=pltpu.VMEM)
    hbm = pl.BlockSpec(memory_space=pltpu.HBM)
    return pl.pallas_call(
        contract_kernel,
        out_shape=jax.ShapeDtypeStruct((row_count * parts * cols, LANES), jnp.bfloat16),
        in_specs=[vmem] * 4 + [hbm],
        out_specs=hbm,
        scratch_shapes=[
            pltpu.VMEM((cols, count, parts * width, LANES), slots.dtype),
            pltpu.VMEM((parts, cols, row_count, LANES), jnp.bfloat16),
            pltpu.VMEM((row_count * parts * cols, LANES), jnp.bfloat16),
            pltpu.SemaphoreType.DMA((cols, count)),
            pltpu.SemaphoreType.DMA((8,)),
        ],
        compiler_params=pltpu.CompilerParams(vmem_limit_bytes=24 * MIB),
    )(
        chosen,
        lhs,
        row_energy,
        col_energy,
        pltpu.with_memory_space_constraint(slots, pltpu.HBM),
    )


def body(
    amplitudes,
    cycle_panels,
    tile_mask,
    panel_slot,
    window_blocks,
    virt_energy,
    row_energy,
    col_energy,
):
    _, _, col_local, width_virt = cycle_panels.shape
    c_local = amplitudes.shape[2]
    occ_rows, occ_summed = tile_mask.shape[:2]
    perm_count = lax.axis_size("perm")
    a_local = amplitudes.shape[1] // perm_count
    p = lax.axis_index("perm")

    width, parts = cycle_panels.shape[1], width_virt // LANES
    as_given = jnp.swapaxes(cycle_panels.reshape(width, col_local, parts, LANES), 1, 2)
    as_given = lax.optimization_barrier(as_given.reshape(-1, LANES))
    by_part = jnp.transpose(as_given.reshape(width, parts, col_local, LANES), (2, 1, 0, 3))
    slots = lax.all_gather(by_part.reshape(-1, LANES), "perm", axis=0)

    blocks = jnp.swapaxes(amplitudes[0].T.reshape(c_local, perm_count, a_local), 0, 1)
    blocks = lax.all_to_all(blocks, "perm", 0, 0, tiled=True)
    blocks, virt_energy, row_energy = lax.optimization_barrier((blocks, virt_energy, row_energy))
    blocks = blocks.reshape(occ_rows, occ_summed, c_local, a_local)
    blocks = jnp.concatenate([blocks[:, k] for k in range(occ_summed)], axis=-1)
    row_virt = lax.dynamic_slice_in_dim(virt_energy, p * a_local, a_local)
    rows = row_virt[:, None] - row_energy[None, :]
    rows = jnp.broadcast_to(rows[..., None], (*rows.shape, LANES)).reshape(-1, LANES)
    columns = virt_energy[None, :] - col_energy[:, None]
    tiles = gather_by_exchange(blocks, ALONG_Z)
    place = CHIPS_Z - 1 - window_blocks
    place = (place << 1 | place >> 2) & (CHIPS_Z - 1)
    tiles = jnp.stack(
        [lax.dynamic_index_in_dim(tiles, place[w], 0, False) for w in range(place.shape[0])]
    )
    tiles, tile_mask, panel_slot, window_blocks = lax.optimization_barrier(
        (tiles, tile_mask, panel_slot, window_blocks)
    )
    tiles = gather_by_exchange(tiles, ALONG_X)
    keep = lax.dynamic_index_in_dim(tile_mask, p // CORES, axis=2, keepdims=False)
    keep = jnp.take(keep, window_blocks, axis=2).transpose(1, 2, 0).reshape(-1, occ_rows)
    keep = jnp.broadcast_to(keep[..., None].astype(jnp.float32), (*keep.shape, LANES))
    chosen = jnp.take(panel_slot.reshape(occ_summed, -1), window_blocks, axis=1).reshape(-1)
    chosen = jnp.broadcast_to(chosen[:, None], (chosen.shape[0], LANES))
    tiles, rows, columns, keep, chosen = lax.optimization_barrier(
        (tiles, rows, columns, keep, chosen)
    )
    lhs = amplitude_rows(keep, tiles)
    result = contract(chosen, lhs, rows, columns, slots)
    result = jnp.swapaxes(result.reshape(-1, parts, col_local, LANES), 1, 2)
    return result.reshape(a_local, occ_rows, col_local, width_virt)


def solution(mesh):
    in_specs = (
        P("perm", None, "summa"),
        P("perm", None, "summa", None),
        P(),
        P(),
        P(),
        P(),
        P(),
        P("summa"),
    )
    out_specs = P("perm", None, "summa", None)
    return jax.shard_map(body, mesh=mesh, in_specs=in_specs, out_specs=out_specs, check_vma=False)
```

```python
import jax
import jax.numpy as jnp
from jax import lax
from jax.experimental import pallas as pl
from jax.experimental.pallas import tpu as pltpu
from jax.sharding import PartitionSpec as P

CORES, CHIPS_Z, CHIPS_X = 2, 8, 4
ORDER_Z, ORDER_X = (7, 3, 6, 2, 5, 1, 4, 0), (3, 1, 2, 0)
ALONG_Z = [[z * CHIPS_X + x for z in ORDER_Z] for x in range(CHIPS_X)]
ALONG_X = [[z * CHIPS_X + x for x in ORDER_X] for z in range(CHIPS_Z)]
MIB = 1024 * 1024
LANES, MXU = 128, 256


def gather_by_exchange(value, groups):
    count = len(groups[0])
    copies = jnp.broadcast_to(value[None], (count, *value.shape))
    return lax.all_to_all(copies, "summa", 0, 0, axis_index_groups=groups, tiled=True)


def together(parts, cols, some):
    count = parts * cols * some
    to = lax.broadcasted_iota(jnp.int32, (count, count), 0)
    of = lax.broadcasted_iota(jnp.int32, (count, count), 1)
    here = of == to % (parts * cols) * some + to // (parts * cols)
    return here.astype(jnp.float32).astype(jnp.bfloat16)


def inverse_kernel(row_energy, col_energy, out):
    parts, cols, _, lanes = out.shape
    for part in range(parts):
        for j in range(cols):
            gap = row_energy[...] + col_energy[pl.ds(j, 1), pl.ds(part * lanes, lanes)]
            out[part, j] = 1.0 / gap


def inverse_gaps(row_energy, col_energy):
    cols, width_virt = col_energy.shape
    vmem = pl.BlockSpec(memory_space=pltpu.VMEM)
    shape = (width_virt // LANES, cols, *row_energy.shape)
    return pl.pallas_call(
        inverse_kernel,
        out_shape=pltpu.VMEM(shape, jnp.float32),
        in_specs=[vmem, vmem],
        out_specs=vmem,
        compiler_params=pltpu.CompilerParams(vmem_limit_bytes=8 * MIB),
    )(row_energy, col_energy)


def rows_kernel(keep, tiles, inverse, out, rows):
    del inverse
    x_count, windows, occ_rows, c_local, lanes = tiles.shape
    half, width = rows.shape[0], x_count * c_local
    summed = lanes // half
    for i in range(occ_rows):
        for w in range(windows):
            tile = jnp.concatenate([tiles[ORDER_X.index(x), w, i] for x in range(x_count)], axis=0)
            tile = tile.astype(jnp.float32).T
            for k in range(summed):
                rows[:, i, pl.ds((k * windows + w) * width, width)] = (
                    tile[k * half : (k + 1) * half] * keep[k * windows + w, pl.ds(i, 1), :]
                )
    out[...] = rows[...].reshape(out.shape).astype(out.dtype)


def amplitude_rows(keep, tiles, inverse):
    x_count, windows, occ_rows, c_local, lanes = tiles.shape
    summed = keep.shape[0] // windows
    half, depth = lanes // summed, summed * windows * x_count * c_local
    vmem = pl.BlockSpec(memory_space=pltpu.VMEM)
    return pl.pallas_call(
        rows_kernel,
        out_shape=jax.ShapeDtypeStruct((half * occ_rows, depth), jnp.bfloat16),
        in_specs=[vmem, vmem, vmem],
        out_specs=vmem,
        scratch_shapes=[pltpu.VMEM((half, occ_rows, depth), jnp.float32)],
        compiler_params=pltpu.CompilerParams(vmem_limit_bytes=16 * MIB),
    )(keep, tiles, pltpu.with_memory_space_constraint(inverse, pltpu.VMEM))


def contract_kernel(
    chosen, lhs, inverse, slots, out, panels, values, done, came, left
):
    row_count, depth = lhs.shape
    cols, count, _, _ = panels.shape
    width = depth // count
    parts = panels.shape[2] // width
    fetches = []
    slot = [jnp.max(chosen[pl.ds(m, 1), :]) for m in range(count)]
    for j in range(cols):
        for m in range(count):
            rows = pl.ds(j * parts * width, parts * width)
            fetches.append(
                pltpu.make_async_copy(slots.at[slot[m], rows], panels.at[j, m], came.at[j, m])
            )
    for fetch in fetches:
        fetch.start()
    beside = MXU // LANES
    some = MXU // (parts * cols)
    order = together(parts, cols, some)
    wide = parts // 2
    steps = [(j, part) for j in range(cols) for part in range(0, parts, wide)]

    def product(j, part):
        if part == 0:
            for fetch in fetches[j * count : (j + 1) * count]:
                fetch.wait()
        rhs = [
            panels[j, :, pl.ds(one * width, width), :].reshape(depth, LANES)
            for one in range(part, part + wide)
        ]
        return jnp.dot(
            lhs[...], jnp.concatenate(rhs, axis=1), preferred_element_type=jnp.float32
        )

    def finish(term, j, part):
        for one in range(wide):
            value = term[:, one * LANES : (one + 1) * LANES] * inverse[part + one, j]
            values[part + one, j] = value.astype(out.dtype)

    term = product(*steps[0])
    for now, later in zip(steps, steps[1:] + [None]):
        ahead = product(*later) if later else None
        finish(term, *now)
        term = ahead
    stores = []
    rows_of = parts * cols
    span = row_count // left.shape[0]
    for m in range(0, row_count, some * beside):
        apart = [
            jnp.concatenate(
                [
                    values[part, j, pl.ds(m + one * some, some), :]
                    for part in range(parts)
                    for j in range(cols)
                ],
                axis=0,
            )
            for one in range(beside)
        ]
        mixed = jnp.dot(order, jnp.concatenate(apart, axis=1), preferred_element_type=jnp.float32)
        mixed = mixed.astype(out.dtype)
        for one in range(beside):
            done[pl.ds((m + one * some) * rows_of, MXU), :] = mixed[:, one * LANES : (one + 1) * LANES]
        if (m + some * beside) % span == 0:
            rows = pl.ds((m + some * beside - span) * rows_of, span * rows_of)
            store = pltpu.make_async_copy(done.at[rows], out.at[rows], left.at[m // span])
            store.start()
            stores.append(store)
    for store in stores:
        store.wait()


def contract(chosen, lhs, inverse, slots):
    row_count, depth = lhs.shape
    parts, cols = inverse.shape[:2]
    width = slots.shape[1] // (parts * cols)
    count = depth // width
    vmem = pl.BlockSpec(memory_space=pltpu.VMEM)
    hbm = pl.BlockSpec(memory_space=pltpu.HBM)
    return pl.pallas_call(
        contract_kernel,
        out_shape=jax.ShapeDtypeStruct((row_count * parts * cols, LANES), jnp.bfloat16),
        in_specs=[vmem] * 3 + [hbm],
        out_specs=hbm,
        scratch_shapes=[
            pltpu.VMEM((cols, count, parts * width, LANES), slots.dtype),
            pltpu.VMEM((parts, cols, row_count, LANES), jnp.bfloat16),
            pltpu.VMEM((row_count * parts * cols, LANES), jnp.bfloat16),
            pltpu.SemaphoreType.DMA((cols, count)),
            pltpu.SemaphoreType.DMA((8,)),
        ],
        compiler_params=pltpu.CompilerParams(vmem_limit_bytes=24 * MIB),
    )(
        chosen,
        lhs,
        pltpu.with_memory_space_constraint(inverse, pltpu.VMEM),
        pltpu.with_memory_space_constraint(slots, pltpu.HBM),
    )


def body(
    amplitudes,
    cycle_panels,
    tile_mask,
    panel_slot,
    window_blocks,
    virt_energy,
    row_energy,
    col_energy,
):
    _, _, col_local, width_virt = cycle_panels.shape
    c_local = amplitudes.shape[2]
    occ_rows, occ_summed = tile_mask.shape[:2]
    perm_count = lax.axis_size("perm")
    a_local = amplitudes.shape[1] // perm_count
    p = lax.axis_index("perm")

    width, parts = cycle_panels.shape[1], width_virt // LANES
    as_given = jnp.swapaxes(cycle_panels.reshape(width, col_local, parts, LANES), 1, 2)
    as_given = lax.optimization_barrier(as_given.reshape(-1, LANES))
    by_part = jnp.transpose(as_given.reshape(width, parts, col_local, LANES), (2, 1, 0, 3))
    slots = lax.all_gather(by_part.reshape(-1, LANES), "perm", axis=0)

    blocks = jnp.swapaxes(amplitudes[0].T.reshape(c_local, perm_count, a_local), 0, 1)
    blocks = lax.all_to_all(blocks, "perm", 0, 0, tiled=True)
    blocks, virt_energy, row_energy = lax.optimization_barrier((blocks, virt_energy, row_energy))
    blocks = blocks.reshape(occ_rows, occ_summed, c_local, a_local)
    blocks = jnp.concatenate([blocks[:, k] for k in range(occ_summed)], axis=-1)
    row_virt = lax.dynamic_slice_in_dim(virt_energy, p * a_local, a_local)
    rows = row_virt[:, None] - row_energy[None, :]
    rows = jnp.broadcast_to(rows[..., None], (*rows.shape, LANES)).reshape(-1, LANES)
    columns = virt_energy[None, :] - col_energy[:, None]
    tiles = gather_by_exchange(blocks, ALONG_Z)
    place = CHIPS_Z - 1 - window_blocks
    place = (place << 1 | place >> 2) & (CHIPS_Z - 1)
    tiles = jnp.stack(
        [lax.dynamic_index_in_dim(tiles, place[w], 0, False) for w in range(place.shape[0])]
    )
    tiles, tile_mask, panel_slot, window_blocks = lax.optimization_barrier(
        (tiles, tile_mask, panel_slot, window_blocks)
    )
    tiles = gather_by_exchange(tiles, ALONG_X)
    keep = lax.dynamic_index_in_dim(tile_mask, p // CORES, axis=2, keepdims=False)
    keep = jnp.take(keep, window_blocks, axis=2).transpose(1, 2, 0).reshape(-1, occ_rows)
    keep = jnp.broadcast_to(keep[..., None].astype(jnp.float32), (*keep.shape, LANES))
    chosen = jnp.take(panel_slot.reshape(occ_summed, -1), window_blocks, axis=1).reshape(-1)
    chosen = jnp.broadcast_to(chosen[:, None], (chosen.shape[0], LANES))
    tiles, keep, chosen = lax.optimization_barrier((tiles, keep, chosen))
    inverse = inverse_gaps(rows, columns)
    lhs = amplitude_rows(keep, tiles, inverse)
    result = contract(chosen, lhs, inverse, slots)
    result = jnp.swapaxes(result.reshape(-1, parts, col_local, LANES), 1, 2)
    return result.reshape(a_local, occ_rows, col_local, width_virt)


def solution(mesh):
    in_specs = (
        P("perm", None, "summa"),
        P("perm", None, "summa", None),
        P(),
        P(),
        P(),
        P(),
        P(),
        P("summa"),
    )
    out_specs = P("perm", None, "summa", None)
    return jax.shard_map(body, mesh=mesh, in_specs=in_specs, out_specs=out_specs, check_vma=False)
```

```python
import jax
import jax.numpy as jnp
from jax import lax
from jax.experimental import pallas as pl
from jax.experimental.pallas import tpu as pltpu
from jax.sharding import PartitionSpec as P

CORES, CHIPS_Z, CHIPS_X = 2, 8, 4
ORDER_Z, ORDER_X = (7, 3, 6, 2, 5, 1, 4, 0), (3, 1, 2, 0)
ALONG_Z = [[z * CHIPS_X + x for z in ORDER_Z] for x in range(CHIPS_X)]
ALONG_X = [[z * CHIPS_X + x for x in ORDER_X] for z in range(CHIPS_Z)]
MIB = 1024 * 1024
LANES, MXU = 128, 256


def gather_by_exchange(value, groups):
    count = len(groups[0])
    copies = jnp.broadcast_to(value[None], (count, *value.shape))
    return lax.all_to_all(copies, "summa", 0, 0, axis_index_groups=groups, tiled=True)


def together(parts, cols, some):
    count = parts * cols * some
    to = lax.broadcasted_iota(jnp.int32, (count, count), 0)
    of = lax.broadcasted_iota(jnp.int32, (count, count), 1)
    here = of == to % (parts * cols) * some + to // (parts * cols)
    return here.astype(jnp.float32).astype(jnp.bfloat16)


def rows_kernel(keep, tiles, out, rows):
    x_count, windows, occ_rows, c_local, lanes = tiles.shape
    half, width = rows.shape[0], x_count * c_local
    summed = lanes // half
    for i in range(occ_rows):
        for w in range(windows):
            tile = jnp.concatenate([tiles[ORDER_X.index(x), w, i] for x in range(x_count)], axis=0)
            tile = tile.astype(jnp.float32).T
            for k in range(summed):
                rows[:, i, pl.ds((k * windows + w) * width, width)] = (
                    tile[k * half : (k + 1) * half] * keep[k * windows + w, pl.ds(i, 1), :]
                )
    out[...] = rows[...].reshape(out.shape).astype(out.dtype)


def amplitude_rows(keep, tiles):
    x_count, windows, occ_rows, c_local, lanes = tiles.shape
    summed = keep.shape[0] // windows
    half, depth = lanes // summed, summed * windows * x_count * c_local
    vmem = pl.BlockSpec(memory_space=pltpu.VMEM)
    return pl.pallas_call(
        rows_kernel,
        out_shape=jax.ShapeDtypeStruct((half * occ_rows, depth), jnp.bfloat16),
        in_specs=[vmem, vmem],
        out_specs=vmem,
        scratch_shapes=[pltpu.VMEM((half, occ_rows, depth), jnp.float32)],
        compiler_params=pltpu.CompilerParams(vmem_limit_bytes=16 * MIB),
    )(keep, tiles)


def contract_kernel(
    chosen, lhs, row_energy, col_energy, slots, out, panels, values, done, came, left
):
    row_count, depth = lhs.shape
    cols, count, _, _ = panels.shape
    width = depth // count
    parts = panels.shape[2] // width
    fetches = []
    slot = [jnp.max(chosen[pl.ds(m, 1), :]) for m in range(count)]
    for j in range(cols):
        for m in range(count):
            rows = pl.ds(j * parts * width, parts * width)
            fetches.append(
                pltpu.make_async_copy(slots.at[slot[m], rows], panels.at[j, m], came.at[j, m])
            )
    for fetch in fetches:
        fetch.start()
    beside = MXU // LANES
    some = MXU // (parts * cols)
    order = together(parts, cols, some)
    stores = []

    def product(j, part, wide, low, size):
        rhs = [
            panels[j, :, pl.ds(one * width, width), :].reshape(depth, LANES)
            for one in range(part, part + wide)
        ]
        return jnp.dot(
            lhs[pl.ds(low, size), :],
            jnp.concatenate(rhs, axis=1),
            preferred_element_type=jnp.float32,
        )

    def finish(term, j, part, wide, low, size):
        for one in range(wide):
            gap = row_energy[pl.ds(low, size), :]
            gap = gap + col_energy[pl.ds(j, 1), pl.ds((part + one) * LANES, LANES)]
            guess = pl.reciprocal(gap, approx=True)
            value = term[:, one * LANES : (one + 1) * LANES] * (guess * (2.0 - gap * guess))
            values[part + one, j, pl.ds(low, size), :] = value.astype(out.dtype)

    def run(steps):
        term = product(*steps[0])
        for now, later in zip(steps, steps[1:] + [None]):
            ahead = product(*later) if later else None
            finish(term, *now)
            term = ahead

    rows_of = parts * cols
    span = row_count // left.shape[0]

    def join(m):
        apart = [
            jnp.concatenate(
                [
                    values[part, j, pl.ds(m + one * some, some), :]
                    for part in range(parts)
                    for j in range(cols)
                ],
                axis=0,
            )
            for one in range(beside)
        ]
        mixed = jnp.dot(order, jnp.concatenate(apart, axis=1), preferred_element_type=jnp.float32)
        mixed = mixed.astype(out.dtype)
        for one in range(beside):
            done[pl.ds((m + one * some) * rows_of, MXU), :] = mixed[:, one * LANES : (one + 1) * LANES]
        if (m + some * beside) % span == 0:
            rows = pl.ds((m + some * beside - span) * rows_of, span * rows_of)
            store = pltpu.make_async_copy(done.at[rows], out.at[rows], left.at[m // span])
            store.start()
            stores.append(store)

    for j in range(cols):
        for fetch in fetches[j * count : (j + 1) * count]:
            fetch.wait()
        if j < cols - 1:
            run([(j, part, parts // 2, 0, row_count) for part in range(0, parts, parts // 2)])
    half = row_count // 2
    first, second = [
        [(cols - 1, part, beside, low, half) for part in range(0, parts, beside)]
        for low in (0, half)
    ]
    run(first)
    groups = list(range(0, half, some * beside))
    each = len(groups) // len(second)
    for n, step in enumerate(second):
        term = product(*step)
        for m in groups[n * each : (n + 1) * each]:
            join(m)
        finish(term, *step)
    for m in range(half, row_count, some * beside):
        join(m)
    for store in stores:
        store.wait()


def contract(chosen, lhs, row_energy, col_energy, slots):
    row_count, depth = lhs.shape
    cols, width_virt = col_energy.shape
    parts = width_virt // LANES
    width = slots.shape[1] // (parts * cols)
    count = depth // width
    vmem = pl.BlockSpec(memory_space=pltpu.VMEM)
    hbm = pl.BlockSpec(memory_space=pltpu.HBM)
    return pl.pallas_call(
        contract_kernel,
        out_shape=jax.ShapeDtypeStruct((row_count * parts * cols, LANES), jnp.bfloat16),
        in_specs=[vmem] * 4 + [hbm],
        out_specs=hbm,
        scratch_shapes=[
            pltpu.VMEM((cols, count, parts * width, LANES), slots.dtype),
            pltpu.VMEM((parts, cols, row_count, LANES), jnp.bfloat16),
            pltpu.VMEM((row_count * parts * cols, LANES), jnp.bfloat16),
            pltpu.SemaphoreType.DMA((cols, count)),
            pltpu.SemaphoreType.DMA((8,)),
        ],
        compiler_params=pltpu.CompilerParams(vmem_limit_bytes=24 * MIB),
    )(
        chosen,
        lhs,
        row_energy,
        col_energy,
        pltpu.with_memory_space_constraint(slots, pltpu.HBM),
    )


def body(
    amplitudes,
    cycle_panels,
    tile_mask,
    panel_slot,
    window_blocks,
    virt_energy,
    row_energy,
    col_energy,
):
    _, _, col_local, width_virt = cycle_panels.shape
    c_local = amplitudes.shape[2]
    occ_rows, occ_summed = tile_mask.shape[:2]
    perm_count = lax.axis_size("perm")
    a_local = amplitudes.shape[1] // perm_count
    p = lax.axis_index("perm")

    width, parts = cycle_panels.shape[1], width_virt // LANES
    as_given = jnp.swapaxes(cycle_panels.reshape(width, col_local, parts, LANES), 1, 2)
    as_given = lax.optimization_barrier(as_given.reshape(-1, LANES))
    by_part = jnp.transpose(as_given.reshape(width, parts, col_local, LANES), (2, 1, 0, 3))
    slots = lax.all_gather(by_part.reshape(-1, LANES), "perm", axis=0)

    blocks = jnp.swapaxes(amplitudes[0].T.reshape(c_local, perm_count, a_local), 0, 1)
    blocks = lax.all_to_all(blocks, "perm", 0, 0, tiled=True)
    blocks, virt_energy, row_energy = lax.optimization_barrier((blocks, virt_energy, row_energy))
    blocks = blocks.reshape(occ_rows, occ_summed, c_local, a_local)
    blocks = jnp.concatenate([blocks[:, k] for k in range(occ_summed)], axis=-1)
    row_virt = lax.dynamic_slice_in_dim(virt_energy, p * a_local, a_local)
    rows = row_virt[:, None] - row_energy[None, :]
    rows = jnp.broadcast_to(rows[..., None], (*rows.shape, LANES)).reshape(-1, LANES)
    columns = virt_energy[None, :] - col_energy[:, None]
    tiles = gather_by_exchange(blocks, ALONG_Z)
    place = CHIPS_Z - 1 - window_blocks
    place = (place << 1 | place >> 2) & (CHIPS_Z - 1)
    tiles = jnp.stack(
        [lax.dynamic_index_in_dim(tiles, place[w], 0, False) for w in range(place.shape[0])]
    )
    tiles, tile_mask, panel_slot, window_blocks = lax.optimization_barrier(
        (tiles, tile_mask, panel_slot, window_blocks)
    )
    tiles = gather_by_exchange(tiles, ALONG_X)
    keep = lax.dynamic_index_in_dim(tile_mask, p // CORES, axis=2, keepdims=False)
    keep = jnp.take(keep, window_blocks, axis=2).transpose(1, 2, 0).reshape(-1, occ_rows)
    keep = jnp.broadcast_to(keep[..., None].astype(jnp.float32), (*keep.shape, LANES))
    chosen = jnp.take(panel_slot.reshape(occ_summed, -1), window_blocks, axis=1).reshape(-1)
    chosen = jnp.broadcast_to(chosen[:, None], (chosen.shape[0], LANES))
    tiles, rows, columns, keep, chosen = lax.optimization_barrier(
        (tiles, rows, columns, keep, chosen)
    )
    lhs = amplitude_rows(keep, tiles)
    result = contract(chosen, lhs, rows, columns, slots)
    result = jnp.swapaxes(result.reshape(-1, parts, col_local, LANES), 1, 2)
    return result.reshape(a_local, occ_rows, col_local, width_virt)


def solution(mesh):
    in_specs = (
        P("perm", None, "summa"),
        P("perm", None, "summa", None),
        P(),
        P(),
        P(),
        P(),
        P(),
        P("summa"),
    )
    out_specs = P("perm", None, "summa", None)
    return jax.shard_map(body, mesh=mesh, in_specs=in_specs, out_specs=out_specs, check_vma=False)
```

```python
import jax
import jax.numpy as jnp
from jax import lax
from jax.experimental import pallas as pl
from jax.experimental.pallas import tpu as pltpu
from jax.sharding import PartitionSpec as P

CORES, CHIPS_Z, CHIPS_X = 2, 8, 4
ORDER_Z, ORDER_X = (7, 3, 6, 2, 5, 1, 4, 0), (3, 1, 2, 0)
ALONG_Z = [[z * CHIPS_X + x for z in ORDER_Z] for x in range(CHIPS_X)]
ALONG_X = [[z * CHIPS_X + x for x in ORDER_X] for z in range(CHIPS_Z)]
MIB = 1024 * 1024
LANES, MXU = 128, 256


def gather_by_exchange(value, groups):
    count = len(groups[0])
    copies = jnp.broadcast_to(value[None], (count, *value.shape))
    return lax.all_to_all(copies, "summa", 0, 0, axis_index_groups=groups, tiled=True)


def together(parts, cols, some):
    count = parts * cols * some
    to = lax.broadcasted_iota(jnp.int32, (count, count), 0)
    of = lax.broadcasted_iota(jnp.int32, (count, count), 1)
    here = of == to % (parts * cols) * some + to // (parts * cols)
    return here.astype(jnp.float32).astype(jnp.bfloat16)


def rows_kernel(keep, tiles, out, rows):
    x_count, windows, occ_rows, c_local, lanes = tiles.shape
    half, width = rows.shape[0], x_count * c_local
    summed = lanes // half
    for i in range(occ_rows):
        for w in range(windows):
            tile = jnp.concatenate([tiles[ORDER_X.index(x), w, i] for x in range(x_count)], axis=0)
            tile = tile.astype(jnp.float32).T
            for k in range(summed):
                rows[:, i, pl.ds((k * windows + w) * width, width)] = (
                    tile[k * half : (k + 1) * half] * keep[k * windows + w, pl.ds(i, 1), :]
                )
    out[...] = rows[...].reshape(out.shape).astype(out.dtype)


def amplitude_rows(keep, tiles):
    x_count, windows, occ_rows, c_local, lanes = tiles.shape
    summed = keep.shape[0] // windows
    half, depth = lanes // summed, summed * windows * x_count * c_local
    vmem = pl.BlockSpec(memory_space=pltpu.VMEM)
    return pl.pallas_call(
        rows_kernel,
        out_shape=jax.ShapeDtypeStruct((half * occ_rows, depth), jnp.bfloat16),
        in_specs=[vmem, vmem],
        out_specs=vmem,
        scratch_shapes=[pltpu.VMEM((half, occ_rows, depth), jnp.float32)],
        compiler_params=pltpu.CompilerParams(vmem_limit_bytes=16 * MIB),
    )(keep, tiles)


def contract_kernel(
    chosen, lhs, row_energy, col_energy, slots, out, panels, values, done, came, left
):
    row_count, depth = lhs.shape
    cols, count, _, _ = panels.shape
    width = depth // count
    parts = panels.shape[2] // width
    fetches = []
    slot = [jnp.max(chosen[pl.ds(m, 1), :]) for m in range(count)]
    for j in range(cols):
        for m in range(count):
            rows = pl.ds(j * parts * width, parts * width)
            fetches.append(
                pltpu.make_async_copy(slots.at[slot[m], rows], panels.at[j, m], came.at[j, m])
            )
    for n, fetch in enumerate(fetches):
        fetch.start(priority=n & 1)
    beside = MXU // LANES
    some = MXU // (parts * cols)
    order = together(parts, cols, some)
    stores = []

    def product(j, part, wide, low, size):
        rhs = [
            panels[j, :, pl.ds(one * width, width), :].reshape(depth, LANES)
            for one in range(part, part + wide)
        ]
        return jnp.dot(
            lhs[pl.ds(low, size), :],
            jnp.concatenate(rhs, axis=1),
            preferred_element_type=jnp.float32,
        )

    def finish(term, j, part, wide, low, size):
        for one in range(wide):
            gap = row_energy[pl.ds(low, size), :]
            gap = gap + col_energy[pl.ds(j, 1), pl.ds((part + one) * LANES, LANES)]
            guess = pl.reciprocal(gap, approx=True)
            value = term[:, one * LANES : (one + 1) * LANES] * (guess * (2.0 - gap * guess))
            values[part + one, j, pl.ds(low, size), :] = value.astype(out.dtype)

    def run(steps):
        term = product(*steps[0])
        for now, later in zip(steps, steps[1:] + [None]):
            ahead = product(*later) if later else None
            finish(term, *now)
            term = ahead

    rows_of = parts * cols
    span = row_count // left.shape[0]

    def join(m):
        apart = [
            jnp.concatenate(
                [
                    values[part, j, pl.ds(m + one * some, some), :]
                    for part in range(parts)
                    for j in range(cols)
                ],
                axis=0,
            )
            for one in range(beside)
        ]
        mixed = jnp.dot(order, jnp.concatenate(apart, axis=1), preferred_element_type=jnp.float32)
        mixed = mixed.astype(out.dtype)
        for one in range(beside):
            done[pl.ds((m + one * some) * rows_of, MXU), :] = mixed[:, one * LANES : (one + 1) * LANES]
        if (m + some * beside) % span == 0:
            rows = pl.ds((m + some * beside - span) * rows_of, span * rows_of)
            store = pltpu.make_async_copy(done.at[rows], out.at[rows], left.at[m // span])
            store.start()
            stores.append(store)

    for j in range(cols):
        for fetch in fetches[j * count : (j + 1) * count]:
            fetch.wait()
        if j < cols - 1:
            run([(j, part, parts // 2, 0, row_count) for part in range(0, parts, parts // 2)])
    half = row_count // 2
    first, second = [
        [(cols - 1, part, beside, low, half) for part in range(0, parts, beside)]
        for low in (0, half)
    ]
    run(first)
    groups = list(range(0, half, some * beside))
    each = len(groups) // len(second)
    for n, step in enumerate(second):
        term = product(*step)
        for m in groups[n * each : (n + 1) * each]:
            join(m)
        finish(term, *step)
    for m in range(half, row_count, some * beside):
        join(m)
    for store in stores:
        store.wait()


def contract(chosen, lhs, row_energy, col_energy, slots):
    row_count, depth = lhs.shape
    cols, width_virt = col_energy.shape
    parts = width_virt // LANES
    width = slots.shape[1] // (parts * cols)
    count = depth // width
    vmem = pl.BlockSpec(memory_space=pltpu.VMEM)
    hbm = pl.BlockSpec(memory_space=pltpu.HBM)
    return pl.pallas_call(
        contract_kernel,
        out_shape=jax.ShapeDtypeStruct((row_count * parts * cols, LANES), jnp.bfloat16),
        in_specs=[vmem] * 4 + [hbm],
        out_specs=hbm,
        scratch_shapes=[
            pltpu.VMEM((cols, count, parts * width, LANES), slots.dtype),
            pltpu.VMEM((parts, cols, row_count, LANES), jnp.bfloat16),
            pltpu.VMEM((row_count * parts * cols, LANES), jnp.bfloat16),
            pltpu.SemaphoreType.DMA((cols, count)),
            pltpu.SemaphoreType.DMA((8,)),
        ],
        compiler_params=pltpu.CompilerParams(vmem_limit_bytes=24 * MIB),
    )(
        chosen,
        lhs,
        row_energy,
        col_energy,
        pltpu.with_memory_space_constraint(slots, pltpu.HBM),
    )


def body(
    amplitudes,
    cycle_panels,
    tile_mask,
    panel_slot,
    window_blocks,
    virt_energy,
    row_energy,
    col_energy,
):
    _, _, col_local, width_virt = cycle_panels.shape
    c_local = amplitudes.shape[2]
    occ_rows, occ_summed = tile_mask.shape[:2]
    perm_count = lax.axis_size("perm")
    a_local = amplitudes.shape[1] // perm_count
    p = lax.axis_index("perm")

    width, parts = cycle_panels.shape[1], width_virt // LANES
    as_given = jnp.swapaxes(cycle_panels.reshape(width, col_local, parts, LANES), 1, 2)
    as_given = lax.optimization_barrier(as_given.reshape(-1, LANES))
    by_part = jnp.transpose(as_given.reshape(width, parts, col_local, LANES), (2, 1, 0, 3))
    slots = lax.all_gather(by_part.reshape(-1, LANES), "perm", axis=0)

    blocks = jnp.swapaxes(amplitudes[0].T.reshape(c_local, perm_count, a_local), 0, 1)
    blocks = lax.all_to_all(blocks, "perm", 0, 0, tiled=True)
    blocks, virt_energy, row_energy = lax.optimization_barrier((blocks, virt_energy, row_energy))
    blocks = blocks.reshape(occ_rows, occ_summed, c_local, a_local)
    blocks = jnp.concatenate([blocks[:, k] for k in range(occ_summed)], axis=-1)
    row_virt = lax.dynamic_slice_in_dim(virt_energy, p * a_local, a_local)
    rows = row_virt[:, None] - row_energy[None, :]
    rows = jnp.broadcast_to(rows[..., None], (*rows.shape, LANES)).reshape(-1, LANES)
    columns = virt_energy[None, :] - col_energy[:, None]
    tiles = gather_by_exchange(blocks, ALONG_Z)
    place = CHIPS_Z - 1 - window_blocks
    place = (place << 1 | place >> 2) & (CHIPS_Z - 1)
    tiles = jnp.stack(
        [lax.dynamic_index_in_dim(tiles, place[w], 0, False) for w in range(place.shape[0])]
    )
    tiles, tile_mask, panel_slot, window_blocks = lax.optimization_barrier(
        (tiles, tile_mask, panel_slot, window_blocks)
    )
    tiles = gather_by_exchange(tiles, ALONG_X)
    keep = lax.dynamic_index_in_dim(tile_mask, p // CORES, axis=2, keepdims=False)
    keep = jnp.take(keep, window_blocks, axis=2).transpose(1, 2, 0).reshape(-1, occ_rows)
    keep = jnp.broadcast_to(keep[..., None].astype(jnp.float32), (*keep.shape, LANES))
    chosen = jnp.take(panel_slot.reshape(occ_summed, -1), window_blocks, axis=1).reshape(-1)
    chosen = jnp.broadcast_to(chosen[:, None], (chosen.shape[0], LANES))
    tiles, rows, columns, keep, chosen = lax.optimization_barrier(
        (tiles, rows, columns, keep, chosen)
    )
    lhs = amplitude_rows(keep, tiles)
    result = contract(chosen, lhs, rows, columns, slots)
    result = jnp.swapaxes(result.reshape(-1, parts, col_local, LANES), 1, 2)
    return result.reshape(a_local, occ_rows, col_local, width_virt)


def solution(mesh):
    in_specs = (
        P("perm", None, "summa"),
        P("perm", None, "summa", None),
        P(),
        P(),
        P(),
        P(),
        P(),
        P("summa"),
    )
    out_specs = P("perm", None, "summa", None)
    return jax.shard_map(body, mesh=mesh, in_specs=in_specs, out_specs=out_specs, check_vma=False)
```
